256 devices in a mesh: pipe: 4 (over x), tensor: 16 (over z, y_lo), dp: 4 (over y_hi, core).
Axes of the slice: x: 4, y: 4 (y_hi: 2, y_lo: 2; y = y_hi * 2 + y_lo), z: 8, core: 2. Of those that a mesh axis runs over, the one named last changes fastest.
Arguments:
- queries: bfloat16 [2048, 4096], P(('pipe', 'dp'), 'tensor'), may hold values from -42 to 42
- encoded_pool: bfloat16 [4096, 8192], P(('pipe', 'dp'), 'tensor'), may hold values from -120 to 120
- choose: int32 [32, 2], P(('pipe', 'dp')), may hold values from 0 to 7, all different within a row
- retrieval_ok: int32 [32], P(('pipe', 'dp')), may hold values 0 or 1
- norm_gain: float32 [4, 8192], P('pipe'), may hold values from 0.4 to 1.6
- w_keyval: bfloat16 [4, 8192, 2, 4096], P('pipe', None, None, 'tensor'), may hold values from -0.0625 to 0.0625
- cotangent: bfloat16 [2048, 4096], P(('pipe', 'dp'), 'tensor'), may hold values from -6 to 6
Outputs:
- attended: bfloat16 [2048, 4096], P(('pipe', 'dp'), 'tensor')
- gain_grad: float32 [4, 8192], P('pipe', 'tensor')
- pool_grad: float32 [4096, 8192], P(('pipe', 'dp'), 'tensor')
The draws below stay inside these ranges and needn't reach their ends.
Inputs may be any that keep to these rules, and one draw needn't show every extreme that they name: `choose`: each row names two different neighbours of its replica's pool of 8; every neighbour is named by some row of the whole array.
All inputs are finite; a program needn't handle non-finite values. No bound on the sum of `retrieval_ok` on one device may be relied on, other than what follows from the above.
Results may differ from the reference program's by a relative error of at most 0.013.
The reference program's roundings to bfloat16 on the way (of `neighbour_rows`, `normed`, `keyval`, `prob_low`, `upstream` and `score_grad`) count: a program that leaves them out, or rounds other values in their place, can miss the bound.
Values may be sent and summed in bfloat16 or wider, within the bound.
No kernel may reach another device: no remote copies, remote signals or barrier semaphores. Data moves between devices by JAX's collectives and lax.ppermute only.
A program may use at most 128 MiB of HBM per device.

```python
import math
import jax
import jax.numpy as jnp
from jax import lax

D = 8192
HS = 128
CL = 64
NL = 128
SPANS = 2
NBR_DEV = 2
HEADS = 32
NBR = 8
GROUPS = 16
N_PIPE = 4
N_DP = 4


def draw_encoded_pool(key, part):
    key = jax.random.fold_in(key, 11)
    first, second, third = jax.random.split(key, 3)
    row_count = N_PIPE * N_DP * NBR_DEV * NL
    base = jnp.clip(jax.random.normal(first, (row_count, D), jnp.float32), -4.0, 4.0)
    row_scale = jnp.exp(jax.random.uniform(second, (row_count, 1), jnp.float32, 0.0, 2.3))
    col_scale = jnp.exp(jax.random.uniform(third, (1, D), jnp.float32, 0.0, 2.3))
    return (base * row_scale * col_scale * 0.29).astype(jnp.bfloat16)


def draw_queries(key, part):
    key = jax.random.fold_in(key, 23)
    first = jax.random.fold_in(key, 0)
    row_count = N_PIPE * N_DP * SPANS * CL
    values = jnp.clip(jax.random.normal(first, (row_count, HEADS * HS), jnp.float32), -4.0, 4.0)
    return values.astype(jnp.bfloat16)


def with_ends(drawn, own_key, least, high):
    shape = drawn.shape
    spot = [jax.random.randint(jax.random.fold_in(own_key, axis), (), 0, shape[axis]) for axis in range(len(shape))]
    drawn = drawn.at[tuple(spot)].set(least)
    longest = shape.index(max(shape))
    spot[longest] = (spot[longest] + 1) % shape[longest]
    return drawn.at[tuple(spot)].set(high)


def levels(stream_key, shape, cuts, low, top_value):
    loudness = 1.0
    for axis_at, parts in cuts:
        heights = jax.random.uniform(jax.random.fold_in(jax.random.fold_in(stream_key, 6), axis_at), (parts,), jnp.float32, low / len(cuts), top_value / len(cuts))
        loudness = loudness * jnp.repeat(jnp.exp(heights), shape[axis_at] // parts).reshape((-1,) + (1,) * (len(shape) - 1 - axis_at))
    return loudness


def picks_of(rng, rows, amount, top, lift):
    order = jax.random.permutation(jax.random.fold_in(rng, 1), amount)
    pull = order
    for power in range(3):
        pull = pull * pull // amount
    pull = pull * lift // amount
    tickets = jax.random.randint(jax.random.fold_in(rng, 2), (rows, amount), 0, 4096) + pull
    holders = jax.random.permutation(jax.random.fold_in(rng, 3), rows)[jnp.arange(amount) % rows]
    tickets = jnp.where(jnp.arange(rows)[:, None] == holders[None, :], 1 << 14, tickets)
    merit = tickets * amount + jnp.arange(amount)
    return lax.top_k(merit.astype(jnp.int32), top)[1].astype(jnp.int32)


def bell_draw(key, dims, spread, most, cuts=(), kind=jnp.bfloat16):
    array = spread * jax.random.normal(key, dims, jnp.float32)
    if cuts:
        array = array * levels(key, dims, cuts, -0.22, 0.18)
    return jnp.clip(array, -most, most).astype(kind)


def setup_inputs(seed: int = 0) -> dict:
    streams_of = jax.random.split(jax.random.key(seed), 8)
    queries = draw_queries(jax.random.fold_in(streams_of[7], 71), 0)
    encoded_pool = draw_encoded_pool(jax.random.fold_in(streams_of[7], 71), 0)
    choose = picks_of(streams_of[2], (GROUPS * SPANS), NBR, 2, 2048)
    retrieval_ok = with_ends((jax.random.randint(streams_of[3], (GROUPS * SPANS,), 0, 4) < 3).astype(jnp.int32), jax.random.fold_in(streams_of[3], 1), 0, 1)
    norm_gain = jnp.clip(1.0 + 0.12 * jax.random.normal(streams_of[4], (N_PIPE, D), jnp.float32), 0.4, 1.6)
    w_keyval = bell_draw(streams_of[5], (N_PIPE, D, 2, HEADS * HS), D ** -0.5, 0.0625, ((0, 4), (3, 16)))
    cotangent = bell_draw(streams_of[6], (GROUPS * SPANS * CL, HEADS * HS), 1.0, 6.0, ((0, 16), (1, 16)))
    return dict(queries=queries, encoded_pool=encoded_pool, choose=choose, retrieval_ok=retrieval_ok, norm_gain=norm_gain, w_keyval=w_keyval, cotangent=cotangent)


epsilon = 1e-05

def reference(queries, encoded_pool, choose, retrieval_ok, norm_gain, w_keyval, cotangent):
    groups = N_PIPE * N_DP
    pool_rep = encoded_pool.reshape(N_PIPE, N_DP, NBR_DEV * NL, D).transpose(1, 0, 2, 3).reshape(N_DP, NBR * NL, D)
    w_flat = w_keyval.reshape(N_PIPE, D, 2 * HEADS * HS)
    query_all = queries.reshape(groups, SPANS, CL, HEADS, HS)
    cot_all = cotangent.reshape(groups, SPANS, CL, HEADS, HS)
    choose_all = choose.reshape(groups, SPANS * 2)
    okay_all = retrieval_ok.reshape(groups, SPANS)
    section_ids = jnp.arange(groups, dtype=jnp.int32) // N_DP
    replica_ids = jnp.arange(groups, dtype=jnp.int32) % N_DP
    score_scale = 1.0 / math.sqrt(HS)
    half_cols = HEADS * HS

    def group_step(items):
        section, replica, query_block, cot_block, picks, okay = items
        own_pool = pool_rep[replica].reshape(NBR, NL, D)
        neighbour_rows = own_pool[picks].reshape(SPANS * 2 * NL, D)
        floats = neighbour_rows.astype(jnp.float32)
        inv_rms = lax.rsqrt(lax.optimization_barrier(jnp.mean(floats * floats, axis=1, keepdims=True)) + epsilon)
        scaled = floats * inv_rms
        gain_row = norm_gain[section][None, :]
        normed = (scaled * gain_row).astype(jnp.bfloat16)
        weights = w_flat[section]
        keyval = jnp.dot(normed, weights, preferred_element_type=jnp.float32).astype(jnp.bfloat16)
        key_block = keyval[:, :half_cols].reshape(SPANS, 2 * NL, HEADS, HS).astype(jnp.float32)
        value_block = keyval[:, half_cols:].reshape(SPANS, 2 * NL, HEADS, HS).astype(jnp.float32)
        query_f = query_block.astype(jnp.float32)
        scores = jnp.einsum('cqhe,cjhe->chqj', query_f, key_block) * score_scale
        attn_prob = jax.nn.softmax(scores, axis=-1)
        prob_low = attn_prob.astype(jnp.bfloat16)
        keep_mask = okay.astype(jnp.float32)[:, None, None, None]
        mixed = jnp.einsum('chqj,cjhe->cqhe', prob_low.astype(jnp.float32), value_block) * keep_mask
        attended = mixed.astype(jnp.bfloat16)
        upstream = (cot_block.astype(jnp.float32) * keep_mask).astype(jnp.bfloat16).astype(jnp.float32)
        prob_grad = jnp.einsum('cqhe,cjhe->chqj', upstream, value_block)
        score_grad = (attn_prob * (prob_grad - lax.optimization_barrier(jnp.sum(prob_grad * attn_prob, axis=-1, keepdims=True))) * score_scale).astype(jnp.bfloat16)
        key_grad = jnp.einsum('chqj,cqhe->cjhe', score_grad.astype(jnp.float32), query_f).astype(jnp.bfloat16)
        value_grad = jnp.einsum('chqj,cqhe->cjhe', prob_low.astype(jnp.float32), upstream).astype(jnp.bfloat16)
        kv_grad = jnp.concatenate([key_grad.reshape(-1, half_cols), value_grad.reshape(-1, half_cols)], axis=1)
        normed_grad = lax.dot_general(kv_grad, weights, (((1,), (1,)), ((), ())), preferred_element_type=jnp.float32)
        row_terms = lax.optimization_barrier(jnp.sum(normed_grad * scaled, axis=0))
        scaled_grad = normed_grad * gain_row
        row_mean = lax.optimization_barrier(jnp.mean(scaled_grad * scaled, axis=1, keepdims=True))
        row_grad = inv_rms * (scaled_grad - scaled * row_mean)
        return (attended, row_terms, row_grad)
    attended, row_terms, row_grad = lax.map(group_step, (section_ids, replica_ids, query_all, cot_all, choose_all, okay_all))
    gain_grad = lax.optimization_barrier(jnp.sum(row_terms.reshape(N_PIPE, N_DP, D), axis=1))
    pieces = row_grad.reshape(groups, SPANS * 2, NL, D)
    pool_sum = jnp.zeros((N_DP, NBR, NL, D), jnp.float32)
    pool_sum = pool_sum.at[replica_ids[:, None], choose_all].add(pieces)
    pool_grad = pool_sum.reshape(N_DP, N_PIPE, NBR_DEV * NL, D).transpose(1, 0, 2, 3).reshape(groups * NBR_DEV * NL, D)
    return (attended.reshape(groups * SPANS * CL, HEADS * HS), gain_grad, pool_grad)
```

```python
import math

import jax
import jax.numpy as jnp
from jax import lax
from jax.sharding import PartitionSpec as P

HS = 128
NL = 128
NBR_DEV = 2
Y = 2

epsilon = 1e-05


def z_shift(count, step):
    ring = count // Y
    return [(i, ((i // Y + step) % ring) * Y + i % Y) for i in range(count)]


def y_swap(count):
    return [(i, i ^ 1) for i in range(count)]


def shift(count, step):
    return [(i, (i + step) % count) for i in range(count)]


def gather_pipe(own, sections):
    half = own.shape[0] // 2
    before = lax.ppermute(own, "pipe", shift(sections, 1))
    after = lax.ppermute(own, "pipe", shift(sections, -1))
    far_low = lax.ppermute(before[:half], "pipe", shift(sections, 1))
    far_high = lax.ppermute(after[half:], "pipe", shift(sections, -1))
    return jnp.concatenate([own, after, far_low, far_high, before], axis=0)


def ring_gather(own, count):
    ring = count // Y
    half = own.shape[0] // 2
    from_low = own
    from_high = own
    got = [(0, own)]
    for step in range(1, ring // 2):
        from_low = lax.ppermute(from_low, "tensor", z_shift(count, 1))
        from_high = lax.ppermute(from_high, "tensor", z_shift(count, -1))
        got.append((-step, from_low))
        got.append((step, from_high))
    low = lax.ppermute(from_low[:half], "tensor", z_shift(count, 1))
    high = lax.ppermute(from_high[half:], "tensor", z_shift(count, -1))
    got.append((ring // 2, jnp.concatenate([low, high], axis=0)))
    return got


def attend(keyval_f32, query, cot, keep):
    spans = 1
    keyval = keyval_f32.astype(jnp.bfloat16)
    half_cols = keyval.shape[1] // 2
    heads = half_cols // HS
    key = keyval[:, :half_cols].reshape(-1, heads, HS)
    value = keyval[:, half_cols:].reshape(-1, heads, HS)
    query = query.reshape(-1, heads, HS)
    score_scale = 1.0 / math.sqrt(HS)
    f32 = dict(preferred_element_type=jnp.float32)
    scores = jnp.einsum("qhe,jhe->hqj", query, key, **f32) * score_scale
    attn_prob = jax.nn.softmax(scores, axis=-1)
    prob_low = attn_prob.astype(jnp.bfloat16)
    attended = (jnp.einsum("hqj,jhe->qhe", prob_low, value, **f32) * keep).astype(jnp.bfloat16)
    upstream = (cot.reshape(query.shape).astype(jnp.float32) * keep).astype(jnp.bfloat16)
    prob_grad = jnp.einsum("qhe,jhe->hqj", upstream, value, **f32)
    score_grad = (
        attn_prob
        * (prob_grad - jnp.sum(prob_grad * attn_prob, axis=-1, keepdims=True))
        * score_scale
    ).astype(jnp.bfloat16)
    key_grad = jnp.einsum("hqj,qhe->jhe", score_grad, query, **f32).astype(jnp.bfloat16)
    value_grad = jnp.einsum("hqj,qhe->jhe", prob_low, upstream, **f32).astype(jnp.bfloat16)
    rows = keyval.shape[0]
    kv_grad = jnp.concatenate(
        [key_grad.reshape(rows, half_cols), value_grad.reshape(rows, half_cols)], axis=1
    )
    stat = jnp.sum(kv_grad.astype(jnp.float32) * keyval_f32, axis=1)
    return attended.reshape(-1, half_cols), kv_grad, stat


def all_sum(x, count):
    x = x + lax.ppermute(x, "tensor", y_swap(count))
    step = 1
    while step < count // Y:
        x = x + lax.ppermute(x, "tensor", [(i, i ^ (step * Y)) for i in range(count)])
        step *= 2
    return x


def after(x, *others):
    return lax.optimization_barrier((x,) + others)[0]


def bf16(x):
    return x.astype(jnp.bfloat16)


def local(queries, encoded_pool, choose, retrieval_ok, norm_gain, w_keyval, cotangent):
    count = lax.axis_size("tensor")
    sections = lax.axis_size("pipe")
    ring = count // Y
    place = lax.axis_index("tensor")
    section = lax.axis_index("pipe")
    own_z, own_y = place // Y, place % Y
    cols = encoded_pool.shape[1]
    width = cols * count
    spans = retrieval_ok.shape[0]

    own_f32 = encoded_pool.astype(jnp.float32)
    squares = jnp.sum(own_f32 * own_f32, axis=1)
    square_sum = all_sum(squares.reshape(NBR_DEV, NL), count)
    hop = [lax.ppermute(square_sum, "pipe", shift(sections, k)) for k in (-1, -2, -3)]
    square_sum = jnp.concatenate([square_sum] + hop, axis=0)
    pool_inv = lax.rsqrt(square_sum / width + epsilon)

    pool_rows = gather_pipe(encoded_pool, sections)
    picks = choose.reshape(-1)
    spot = lax.rem(picks // NBR_DEV - section + sections, sections) * NBR_DEV + picks % NBR_DEV
    picked = pool_rows.reshape(-1, NL, cols)[spot].reshape(-1, cols)
    inv = pool_inv[spot].reshape(-1, 1)
    rows = picked.shape[0] // spans

    weights = after(w_keyval, picked)[0].reshape(width, -1)
    gain = norm_gain

    def block_of(distance, other):
        at_z = lax.rem(own_z + distance + ring, ring)
        at_y = (1 - own_y) if other else own_y
        return (at_z * Y + at_y) * cols

    def weight_rows(distance, other):
        return lax.dynamic_slice_in_dim(weights, block_of(distance, other), cols, 0)

    def product(block, inverse, distance, other):
        gain_cols = lax.dynamic_slice_in_dim(gain, block_of(distance, other), cols, 1)
        normed = bf16(block.astype(jnp.float32) * inverse * gain_cols)
        return jnp.dot(normed, weight_rows(distance, other), preferred_element_type=jnp.float32)

    first, second = picked[:rows], picked[rows:]
    inv_first, inv_second = inv[:rows], inv[rows:]
    partner = lax.ppermute(first, "tensor", y_swap(count))
    own_blocks = dict(ring_gather(picked, count))
    partner_blocks = dict(ring_gather(partner, count))
    keyval_first = 0.0
    keyval_second = 0.0
    for group in ((0,), (-1, 1), (-2, 2), (-3, 3), (4,)):
        sent = jnp.concatenate([own_blocks[d][rows:] for d in group], axis=0)
        crossed = lax.ppermute(sent, "tensor", y_swap(count))
        for i, d in enumerate(group):
            keyval_first = keyval_first + product(own_blocks[d][:rows], inv_first, d, False)
            keyval_first = keyval_first + product(partner_blocks[d], inv_first, d, True)
            keyval_second = keyval_second + product(own_blocks[d][rows:], inv_second, d, False)
            block = crossed[i * rows : (i + 1) * rows]
            keyval_second = keyval_second + product(block, inv_second, d, True)

    keep = retrieval_ok.astype(jnp.float32)
    tokens = queries.shape[0] // spans
    att_a, grad_a, stat_a = attend(keyval_first, queries[:tokens], cotangent[:tokens], keep[0])
    att_b, grad_b, stat_b = attend(keyval_second, queries[tokens:], cotangent[tokens:], keep[1])
    attended = jnp.concatenate([att_a, att_b], axis=0)
    stats = all_sum(jnp.concatenate([stat_a, stat_b]).reshape(-1, NL), count)
    row_mean = (stats / width).reshape(-1, 1)

    def back(grad, distance, other):
        return lax.dot_general(
            grad,
            weight_rows(distance, other),
            (((1,), (1,)), ((), ())),
            preferred_element_type=jnp.float32,
        )

    z_up, z_down = z_shift(count, 1), z_shift(count, -1)

    crossed = {}
    gates = [grad_b, grad_b]
    for group in ((4,), (3, -3), (2, -2), (1, -1), (0,)):
        grad = after(grad_b, gates[-2])
        sent = jnp.concatenate([bf16(back(grad, d, True)) for d in group], axis=0)
        got = lax.ppermute(sent, "tensor", y_swap(count))
        gates.append(got)
        for i, d in enumerate(group):
            crossed[d] = got[i * rows : (i + 1) * rows]

    half = rows // 2
    far = bf16(back(grad_a, 4, True))
    v_up = lax.ppermute(far[:half], "tensor", z_up)
    v_down = lax.ppermute(far[half:], "tensor", z_down)
    u_up = lax.ppermute(bf16(back(grad_a, 4, False)), "tensor", z_up)
    u_down = lax.ppermute(bf16(back(grad_b, 4, False) + crossed[4]), "tensor", z_down)
    for d in (3, 2, 1):
        grad = after(grad_a, v_up, v_down)
        ahead, behind = back(grad, d, True), back(grad, -d, True)
        if d == 3:
            ahead = jnp.concatenate([ahead[:half] + v_up, ahead[half:]], axis=0)
            behind = jnp.concatenate([behind[:half], behind[half:] + v_down], axis=0)
        else:
            ahead, behind = ahead + v_up, behind + v_down
        v_up = lax.ppermute(bf16(ahead), "tensor", z_up)
        v_down = lax.ppermute(bf16(behind), "tensor", z_down)
        g_a, g_b = after(grad_a, u_up, u_down), after(grad_b, u_up, u_down)
        ahead_a, ahead_b = back(g_a, d, False), back(g_b, d, False) + crossed[d]
        behind_a, behind_b = back(g_a, -d, False), back(g_b, -d, False) + crossed[-d]
        ahead_a = ahead_a + u_up[:rows]
        behind_b = behind_b + u_down[-rows:]
        if d < 3:
            ahead_b = ahead_b + u_up[rows:]
            behind_a = behind_a + u_down[:rows]
        u_up = lax.ppermute(
            jnp.concatenate([bf16(ahead_a), bf16(ahead_b)], axis=0), "tensor", z_up
        )
        u_down = lax.ppermute(
            jnp.concatenate([bf16(behind_a), bf16(behind_b)], axis=0), "tensor", z_down
        )
    sum_other = back(after(grad_a, v_up, v_down), 0, True) + v_up + v_down
    swapped = lax.ppermute(bf16(sum_other), "tensor", y_swap(count))
    g_a, g_b = after(grad_a, u_up, u_down), after(grad_b, u_up, u_down)
    sum_first = back(g_a, 0, False) + u_up[:rows] + u_down[:rows] + swapped
    sum_second = back(g_b, 0, False) + u_up[rows:] + u_down[rows:] + crossed[0]
    summed = jnp.concatenate([sum_first, sum_second], axis=0)

    scaled = picked.astype(jnp.float32) * inv
    gain_cols = lax.dynamic_slice_in_dim(gain, place * cols, cols, 1)
    back_rows = inv * (summed * gain_cols - scaled * row_mean)
    share = jnp.sum(summed * scaled, axis=0, keepdims=True)
    replicas = lax.axis_size("dp")
    share = share + lax.ppermute(share, "dp", [(i, i ^ 1) for i in range(replicas)])
    share = share + lax.ppermute(share, "dp", [(i, i ^ 2) for i in range(replicas)])

    pieces = back_rows.reshape(-1, NL, cols)

    def pool_part(d):
        at = lax.rem(section + d, sections) * NBR_DEV
        out = []
        for slot in range(NBR_DEV):
            total = 0.0
            for k in range(pieces.shape[0]):
                total = total + jnp.where(picks[k] == at + slot, pieces[k], 0.0)
            out.append(total)
        return jnp.concatenate(out, axis=0)

    far = bf16(pool_part(2))
    half = far.shape[0] // 2
    up = lax.ppermute(far[:half], "pipe", shift(sections, 1))
    down = lax.ppermute(far[half:], "pipe", shift(sections, -1))
    ahead, behind = pool_part(1), pool_part(3)
    ahead = jnp.concatenate([ahead[:half] + up, ahead[half:]], axis=0)
    behind = jnp.concatenate([behind[:half], behind[half:] + down], axis=0)
    up = lax.ppermute(bf16(ahead), "pipe", shift(sections, 1))
    down = lax.ppermute(bf16(behind), "pipe", shift(sections, -1))
    pool_grad = pool_part(0) + up + down
    return (attended, share, pool_grad)


def solution(mesh):
    return jax.shard_map(
        local,
        mesh=mesh,
        in_specs=(
            P(("pipe", "dp"), "tensor"),
            P(("pipe", "dp"), "tensor"),
            P(("pipe", "dp"), None),
            P(("pipe", "dp")),
            P("pipe", None),
            P("pipe", None, None, "tensor"),
            P(("pipe", "dp"), "tensor"),
        ),
        out_specs=(P(("pipe", "dp"), "tensor"), P("pipe", "tensor"), P(("pipe", "dp"), "tensor")),
        check_vma=False,
    )
```

```python
import functools
import math

import jax
import jax.numpy as jnp
from jax import lax
from jax.experimental import pallas as pl
from jax.experimental.pallas import tpu as pltpu
from jax.sharding import PartitionSpec as P

HS = 128
NL = 128
NBR_DEV = 2
Y = 2
SLAB = 16
MIB = 1 << 20
FULL = 40 * MIB

epsilon = 1e-05
VMEM = pl.BlockSpec(memory_space=pltpu.VMEM)
SMEM = pl.BlockSpec(memory_space=pltpu.SMEM)
HBM = pl.BlockSpec(memory_space=pltpu.HBM)
COST = pl.CostEstimate(flops=2 * 10**10, bytes_accessed=1, transcendentals=0)
NT = (((1,), (1,)), ((), ()))
NN = (((1,), (0,)), ((), ()))
TN = (((0,), (0,)), ((), ()))


def bf16(x):
    return x.astype(jnp.bfloat16)


def f32(x):
    return x.astype(jnp.float32)


def dot(a, b, dims):
    return lax.dot_general(a, b, dims, preferred_element_type=jnp.float32)


def z_shift(count, step):
    ring = count // Y
    return [(i, ((i // Y + step) % ring) * Y + i % Y) for i in range(count)]


def y_swap(count):
    return [(i, i ^ 1) for i in range(count)]


def shift(count, step):
    return [(i, (i + step) % count) for i in range(count)]


def after(x, *others):
    return lax.optimization_barrier((x,) + others)[0]


def gather_pipe(own, sections, weights):
    half = own.shape[0] // 2
    up, down = shift(sections, 1), shift(sections, -1)
    before, behind = lax.ppermute(own, "pipe", up), lax.ppermute(own, "pipe", down)
    far_low = lax.ppermute(after(before[:half], weights), "pipe", up)
    far_high = lax.ppermute(after(behind[half:], weights), "pipe", down)
    return jnp.concatenate([own, behind, far_low, far_high, before], axis=0)


def encode(stat):
    high = bf16(stat)
    rest = stat - f32(high)
    middle = bf16(rest)
    low = bf16(rest - f32(middle))
    row = lax.broadcasted_iota(jnp.int32, (SLAB, stat.shape[1]), 0)
    slab = jnp.where(row == 0, f32(high), jnp.where(row == 1, f32(middle), f32(low)))
    return bf16(jnp.where(row < 3, slab, 0.0))


def decode(slab):
    return jnp.sum(f32(slab), axis=0, keepdims=True)


def squares_kernel(copies, sources, *refs):
    out = refs[-1]
    if len(refs) > sources + 1:
        out[...] = refs[sources][...]
    else:
        out[...] = jnp.zeros_like(out)
    for a, src, n, _, dst in copies:
        for r in range(0, n, 128):
            part = out[dst + r : dst + r + 128]
            for c in range(0, refs[a].shape[1], 128):
                x = f32(refs[a][src + r : src + r + 128, c : c + 128])
                part = part + x * x
            out[dst + r : dst + r + 128] = part


def add_squares(sources, copies, before, total):
    return pl.pallas_call(
        functools.partial(squares_kernel, copies, len(sources)),
        out_shape=pltpu.VMEM((total, 128), jnp.float32),
        in_specs=[VMEM] * (len(sources) + len(before)),
        out_specs=VMEM,
        compiler_params=pltpu.CompilerParams(vmem_limit_bytes=16 * MIB),
        cost_estimate=COST,
    )(*sources, *before)


def forward_kernel(copies, width, *refs):
    ids, okay, gain, query, cot, squares = refs[:6]
    sources = refs[6:-11]
    weights, attended, *grads, slab, inv, ws, xs, acc, x_sem, w_sem = refs[-11:]
    total, cols = acc.shape
    turn = []
    for copy in copies:
        if copy[3] not in turn:
            turn.append(copy[3])
    fetches = {k: [] for k in turn}
    for i, (a, src, n, k, dst) in enumerate(copies):
        x = pltpu.make_async_copy(
            sources[a].at[pl.ds(src, n)], xs.at[k, pl.ds(dst, n)], x_sem.at[i]
        )
        fetches[k].append(x)
    for k in turn:
        at = pl.multiple_of(ids[k] * cols, cols)
        w = pltpu.make_async_copy(weights.at[pl.ds(at, cols)], ws.at[k], w_sem.at[k])
        fetches[k].append(w)
        for fetch in fetches[k]:
            fetch.start()
    mean = jnp.sum(squares[...], axis=1, keepdims=True) / width
    inv[...] = jnp.broadcast_to(lax.rsqrt(mean + epsilon), inv.shape)
    acc[...] = jnp.zeros_like(acc)
    for k in turn:
        for fetch in fetches[k]:
            fetch.wait()
        scaled = f32(xs[k]) * inv[:, :1]
        acc[...] += dot(bf16(scaled * gain[pl.ds(ids[k], 1), :]), ws[k], NN)

    heads = cols // (2 * HS)
    scale = 1.0 / math.sqrt(HS)
    spans = len(grads)
    rows, tokens = total // spans, query.shape[0] // spans
    for c in range(spans):
        keep = okay[c].astype(jnp.float32)
        at, tok = c * rows, c * tokens
        for h in range(heads):
            lo, hi = h * HS, (heads + h) * HS
            key = bf16(acc[at : at + rows, lo : lo + HS])
            value = bf16(acc[at : at + rows, hi : hi + HS])
            q = query[tok : tok + tokens, lo : lo + HS]
            up = bf16(f32(cot[tok : tok + tokens, lo : lo + HS]) * keep)
            scores = dot(q, key, NT) * scale
            e = jnp.exp(scores - jnp.max(scores, axis=1, keepdims=True))
            prob = e / jnp.sum(e, axis=1, keepdims=True)
            low = bf16(prob)
            attended[tok : tok + tokens, lo : lo + HS] = bf16(dot(low, value, NN) * keep)
            prob_grad = dot(up, value, NT)
            inner = jnp.sum(prob_grad * prob, axis=1, keepdims=True)
            score_grad = bf16(prob * (prob_grad - inner) * scale)
            grads[c][:, lo : lo + HS] = bf16(dot(score_grad, q, TN))
            grads[c][:, hi : hi + HS] = bf16(dot(low, up, TN))
        stat = jnp.sum(f32(grads[c][...]) * acc[at : at + rows], axis=1, keepdims=True)
        slab[:, at : at + rows] = encode(jnp.broadcast_to(stat, (rows, 128)).T[:1])


def forward(ids, okay, gain, query, cot, squares, sources, copies, weights):
    width, cols = weights.shape
    count = width // cols
    spans = okay.shape[0]
    total = squares.shape[0]
    return pl.pallas_call(
        functools.partial(forward_kernel, copies, width),
        out_shape=(
            jax.ShapeDtypeStruct(query.shape, jnp.bfloat16),
            *[pltpu.VMEM((total // spans, cols), jnp.bfloat16) for _ in range(spans)],
            pltpu.VMEM((SLAB, total), jnp.bfloat16),
            pltpu.VMEM((total, 128), jnp.float32),
            pltpu.VMEM((count, cols, cols), jnp.bfloat16),
        ),
        in_specs=[SMEM, SMEM] + [VMEM] * 4 + [HBM] * (len(sources) + 1),
        out_specs=(VMEM,) * (spans + 4),
        scratch_shapes=[
            pltpu.VMEM((count, total, cols), jnp.bfloat16),
            pltpu.VMEM((total, cols), jnp.float32),
            pltpu.SemaphoreType.DMA((len(copies),)),
            pltpu.SemaphoreType.DMA((count,)),
        ],
        compiler_params=pltpu.CompilerParams(vmem_limit_bytes=FULL),
        cost_estimate=COST,
    )(ids, okay, gain, query, cot, squares, *sources, weights)


def step_kernel(outs, spans, arrays, *refs):
    grads, weights, given, out_refs = refs[:spans], refs[spans], refs[spans + 1 :][:arrays], refs[spans + 1 + arrays :]
    for out, out_ref in zip(outs, out_refs):
        row = 0
        for s in out:
            if s[0] == "sum":
                _, span, first, n, k, adds = s
                total = dot(grads[span][first : first + n], weights[k], NT)
                for a, r in adds:
                    total = total + f32(given[a][r : r + n])
                out_ref[row : row + n] = total.astype(out_ref.dtype)
            elif s[0] == "copy":
                _, a, r, n = s
                out_ref[row : row + n] = given[a][r : r + n]
            else:
                _, (a, r), (b, t) = s
                n = SLAB
                pair = decode(given[a][r : r + n]) + decode(given[b][t : t + n])
                out_ref[row : row + n] = encode(pair)
            row += n


def step(grads, weights, outs, arrays, dtype):
    cols = grads[0].shape[1]
    size = {"sum": lambda s: s[3], "copy": lambda s: s[3], "pair": lambda s: SLAB}
    heights = [sum(size[s[0]](s) for s in out) for out in outs]
    return pl.pallas_call(
        functools.partial(step_kernel, outs, len(grads), len(arrays)),
        out_shape=[pltpu.VMEM((n, cols), dtype) for n in heights],
        in_specs=[VMEM] * (len(grads) + 1 + len(arrays)),
        out_specs=[VMEM] * len(outs),
        compiler_params=pltpu.CompilerParams(vmem_limit_bytes=16 * MIB),
        cost_estimate=COST,
    )(*grads, weights, *arrays)


def tail_kernel(slabs, sections, width, *refs):
    ids, choose, gain, inv, picked, before, swapped, u_up, u_down = refs[:9]
    hops = refs[7:-7]
    share, far, ahead, behind, own, total, back = refs[-7:]
    rows, cols = total.shape
    half = rows // 2
    stat = jnp.zeros((1, rows), jnp.float32)
    for a, r in slabs:
        stat = stat + decode(hops[a][r : r + SLAB])
    mean = jnp.broadcast_to(stat / width, (128, rows)).T
    gain_row = gain[pl.ds(ids[0], 1), :]
    sums = jnp.zeros((1, cols), jnp.float32)
    for c in range(0, rows, NL):
        grads = before[c : c + NL] + f32(u_up[c : c + NL]) + f32(u_down[c : c + NL])
        if c < half:
            grads = grads + f32(swapped[c : c + NL])
        inverse = inv[c : c + NL, :1]
        scaled = f32(picked[c : c + NL]) * inverse
        sums = sums + jnp.sum(grads * scaled, axis=0, keepdims=True)
        back[c : c + NL] = inverse * (grads * gain_row - scaled * mean[c : c + NL, :1])
    share[...] = sums
    section = ids[ids.shape[0] - 1]
    for d, out in enumerate((own, ahead, far, behind)):
        for slot in range(NBR_DEV):
            n = lax.rem(section + d, sections) * NBR_DEV + slot
            part = jnp.zeros((NL, cols), jnp.float32)
            for k in range(rows // NL):
                part = part + jnp.where(choose[k] == n, back[k * NL : (k + 1) * NL], 0.0)
            out[slot * NL : (slot + 1) * NL] = part.astype(out.dtype)


def tail(ids, choose, gain, inv, picked, before, swapped, u_up, u_down, hops, slabs, sections):
    rows, cols = before.shape
    block = (NBR_DEV * NL, cols)
    return pl.pallas_call(
        functools.partial(tail_kernel, slabs, sections, gain.size),
        out_shape=(
            pltpu.VMEM((1, cols), jnp.float32),
            pltpu.VMEM(block, jnp.bfloat16),
            pltpu.VMEM(block, jnp.float32),
            pltpu.VMEM(block, jnp.float32),
            pltpu.VMEM(block, jnp.float32),
        ),
        in_specs=[SMEM, SMEM] + [VMEM] * (7 + len(hops)),
        out_specs=(VMEM,) * 5,
        scratch_shapes=[
            pltpu.VMEM((rows, cols), jnp.float32),
            pltpu.VMEM((rows, cols), jnp.float32),
        ],
        compiler_params=pltpu.CompilerParams(vmem_limit_bytes=16 * MIB),
        cost_estimate=COST,
    )(ids, choose, gain, inv, picked, before, swapped, u_up, u_down, *hops)


def local(queries, encoded_pool, choose, retrieval_ok, norm_gain, w_keyval, cotangent):
    count = lax.axis_size("tensor")
    sections = lax.axis_size("pipe")
    ring = count // Y
    reach = ring // 2
    place = lax.axis_index("tensor")
    section = lax.axis_index("pipe")
    cols = encoded_pool.shape[1]
    width = cols * count
    spans = retrieval_ok.shape[0]
    z_up, z_down, y_cross = z_shift(count, 1), z_shift(count, -1), y_swap(count)

    def send(x, perm):
        return lax.ppermute(x, "tensor", perm)

    order = jnp.arange(count + 1, dtype=jnp.int32)
    at_z = (place // Y + order // Y) % ring
    ids = jnp.where(order == count, section, at_z * Y + (place % Y + order) % Y)
    gain = norm_gain.reshape(count, cols)

    picks = choose.reshape(-1)
    spot = (picks // NBR_DEV - section + sections) % sections * NBR_DEV + picks % NBR_DEV
    weights = w_keyval[0].reshape(width, -1)
    pool_rows = gather_pipe(encoded_pool, sections, weights)
    picked = pool_rows.reshape(-1, NL, cols)[spot].reshape(-1, cols)
    total = picked.shape[0]
    rows = total // spans

    sources, copies = [], []
    squares = []

    def use(*given):
        nonlocal squares
        fresh = []
        for i, (array, pieces) in enumerate(given):
            copies.extend((len(sources),) + piece for piece in pieces)
            fresh.extend((i,) + piece for piece in pieces)
            sources.append(array)
        squares = [add_squares([array for array, _ in given], tuple(fresh), squares, total)]

    half = rows // 2
    far = 2 * reach
    u_low, u_high = send(picked, z_up), send(picked, z_down)
    partner = send(picked[:rows], y_cross)
    crossing = (send(picked[rows:], y_cross), [(0, rows, 1, rows)])
    use((picked, [(0, total, 0, 0)]), (partner, [(0, rows, 1, 0)]))
    v_low = v_high = after(partner, squares[0])
    for d in range(1, reach + 1):
        low_k, high_k = 2 * (ring - d), 2 * d
        v_low, v_high = send(v_low, z_up), send(v_high, z_down)
        if d == reach:
            use((v_low, [(0, half, far + 1, 0)]), (v_high, [(0, half, far + 1, half)]))
            use((u_low, [(0, rows, far, 0)]), (u_high, [(0, rows, far, rows)]), crossing)
            crossing = send(after(u_high, squares[0]), y_cross)
            break
        use((u_low, [(0, total, low_k, 0)]), (u_high, [(0, total, high_k, 0)]), crossing)
        sent = jnp.concatenate([u_low[rows:], u_high[rows:]], axis=0)
        if d == reach - 1:
            u_low, u_high = u_low[:rows], u_high[rows:]
        u_low = send(after(u_low, squares[0]), z_up)
        u_high = send(after(u_high, squares[0]), z_down)
        crossing = (
            send(after(sent, squares[0]), y_cross),
            [(0, rows, low_k + 1, rows), (rows, rows, high_k + 1, rows)],
        )
        use((v_low, [(0, rows, low_k + 1, 0)]), (v_high, [(0, rows, high_k + 1, 0)]))
        if d == reach - 1:
            v_low, v_high = v_low[:half], v_high[half:]
        v_low, v_high = after(v_low, squares[0]), after(v_high, squares[0])

    use((crossing, [(0, rows, far + 1, rows)]))
    attended, grad_a, grad_b, slab, inv, w_here = forward(
        ids, retrieval_ok, gain, queries, cotangent, squares[0], sources, tuple(copies), weights
    )

    grads = [grad_a, grad_b]
    last_step = [grad_a]

    def back(outs, arrays, *gates, dtype=jnp.bfloat16):
        held = [after(grad, last_step[0], *gates) for grad in grads]
        got = step(held, w_here, outs, arrays, dtype)
        last_step[0] = got[0]
        return got

    crossed = {}

    def cross(d, *gates):
        ks = [2 * d + 1] if d == 0 else [2 * d + 1, 2 * (ring - d) + 1]
        (got,) = back([[("sum", 1, 0, rows, k, []) for k in ks]], [], *gates)
        got = send(got, y_cross)
        for i, k in enumerate(ks):
            crossed[k - 1] = (got, i * rows)
        return got

    v_up, v_down, u_up = back(
        [
            [("sum", 0, 0, half, far + 1, [])],
            [("sum", 0, half, half, far + 1, [])],
            [("sum", 0, 0, rows, far, [])],
        ],
        [],
    )
    v_up, v_down = send(v_up, z_up), send(v_down, z_down)
    u_up = send(u_up, z_up)
    (c_far,) = back([[("sum", 1, 0, rows, far + 1, []), ("copy", 0, 0, SLAB)]], [slab])
    c_far = send(c_far, y_cross)
    c_last = cross(reach - 1)

    def v_step(d, v_up, v_down):
        ahead, behind = 2 * d + 1, 2 * (ring - d) + 1
        if d == 0:
            outs = [[("sum", 0, 0, rows, 1, [(0, 0), (1, 0)])]]
            return send(back(outs, [v_up, v_down])[0], y_cross), None
        if d == reach - 1:
            outs = [
                [("sum", 0, 0, half, ahead, [(0, 0)]), ("sum", 0, half, half, ahead, [])],
                [("sum", 0, 0, half, behind, []), ("sum", 0, half, half, behind, [(1, 0)])],
            ]
        else:
            outs = [
                [("sum", 0, 0, rows, ahead, [(0, 0)])],
                [("sum", 0, 0, rows, behind, [(1, 0)])],
            ]
        v_up, v_down = back(outs, [v_up, v_down])
        return send(v_up, z_up), send(v_down, z_down)

    v_up, v_down = v_step(reach - 1, v_up, v_down)
    (u_sent,) = back(
        [[("sum", 1, 0, rows, far, [(1, 0)]), ("pair", (0, 0), (1, rows))]], [slab, c_far]
    )
    u_down = send(u_sent, z_down)
    hops, slabs = [u_sent, u_down], [(0, rows), (1, rows)]
    for d in range(reach - 1, 0, -1):
        v_up, v_down = v_step(d - 1, v_up, v_down)
        c_last = cross(d - 1, c_last)
        ahead, behind = 2 * d, 2 * (ring - d)
        c_ahead, c_behind = (2, crossed[ahead][1]), (3, crossed[behind][1])
        arrays = [u_up, u_down, crossed[ahead][0], crossed[behind][0]]
        if d == reach - 1:
            arrays.append(u_sent)
            outs = [
                [
                    ("sum", 0, 0, rows, ahead, [(0, 0)]),
                    ("sum", 1, 0, rows, ahead, [c_ahead]),
                    ("copy", 4, rows, SLAB),
                ],
                [
                    ("sum", 0, 0, rows, behind, []),
                    ("sum", 1, 0, rows, behind, [(1, 0), c_behind]),
                    ("copy", 1, rows, SLAB),
                ],
            ]
        else:
            outs = [
                [
                    ("sum", 0, 0, rows, ahead, [(0, 0)]),
                    ("sum", 1, 0, rows, ahead, [(0, rows), c_ahead]),
                    ("copy", 0, total, SLAB),
                ],
                [
                    ("sum", 0, 0, rows, behind, [(1, 0)]),
                    ("sum", 1, 0, rows, behind, [(1, rows), c_behind]),
                    ("copy", 1, total, SLAB),
                ],
            ]
        u_up, u_down = back(outs, arrays)
        u_up, u_down = send(u_up, z_up), send(u_down, z_down)
        hops += [u_up, u_down]
        slabs += [(len(hops) - 2, total), (len(hops) - 1, total)]
    swapped = v_up
    (before,) = back(
        [[("sum", 0, 0, rows, 0, []), ("sum", 1, 0, rows, 0, [(0, 0)])]],
        [crossed[0][0]],
        dtype=jnp.float32,
    )
    hops = [u_up, u_down] + hops[:-2]
    slabs = [((a + 2) % len(hops), r) for a, r in slabs]
    share, far, ahead, behind, own = tail(
        ids, picks, gain, inv, picked, before, swapped, u_up, u_down,
        hops[2:], tuple(slabs), sections,
    )

    half = far.shape[0] // 2
    up = lax.ppermute(far[:half], "pipe", shift(sections, 1))
    down = lax.ppermute(far[half:], "pipe", shift(sections, -1))
    replicas = lax.axis_size("dp")
    share = after(share, up)
    others = [
        lax.ppermute(share, "dp", [(i, i ^ k) for i in range(replicas)]) for k in range(1, replicas)
    ]
    share = sum(others, share)
    ahead = jnp.concatenate([ahead[:half] + up, ahead[half:]], axis=0)
    behind = jnp.concatenate([behind[:half], behind[half:] + down], axis=0)
    up = lax.ppermute(bf16(ahead), "pipe", shift(sections, 1))
    down = lax.ppermute(bf16(behind), "pipe", shift(sections, -1))
    pool_grad = own + up + down
    return (attended, share, pool_grad)


def solution(mesh):
    return jax.shard_map(
        local,
        mesh=mesh,
        in_specs=(
            P(("pipe", "dp"), "tensor"),
            P(("pipe", "dp"), "tensor"),
            P(("pipe", "dp"), None),
            P(("pipe", "dp")),
            P("pipe", None),
            P("pipe", None, None, "tensor"),
            P(("pipe", "dp"), "tensor"),
        ),
        out_specs=(P(("pipe", "dp"), "tensor"), P("pipe", "tensor"), P(("pipe", "dp"), "tensor")),
        check_vma=False,
    )
```

```python
import functools
import math

import jax
import jax.numpy as jnp
from jax import lax
from jax.experimental import pallas as pl
from jax.experimental.pallas import tpu as pltpu
from jax.sharding import PartitionSpec as P

HS = 128
NL = 128
NBR_DEV = 2
Y = 2
SLAB = 16
GROUP = 4
MIB = 1 << 20

epsilon = 1e-05
VMEM = pl.BlockSpec(memory_space=pltpu.VMEM)
SMEM = pl.BlockSpec(memory_space=pltpu.SMEM)
HBM = pl.BlockSpec(memory_space=pltpu.HBM)
ANY = pl.BlockSpec(memory_space=pl.ANY)
COST = pl.CostEstimate(flops=4 * 10**9, bytes_accessed=1, transcendentals=0)
LIGHT = pl.CostEstimate(flops=1, bytes_accessed=1, transcendentals=0)
NT = (((1,), (1,)), ((), ()))
NN = (((1,), (0,)), ((), ()))
TN = (((0,), (0,)), ((), ()))


def bf16(x):
    return x.astype(jnp.bfloat16)


def f32(x):
    return x.astype(jnp.float32)


def dot(a, b, dims):
    return lax.dot_general(a, b, dims, preferred_element_type=jnp.float32)


def z_shift(count, step):
    ring = count // Y
    return [(i, ((i // Y + step) % ring) * Y + i % Y) for i in range(count)]


def y_swap(count):
    return [(i, i ^ 1) for i in range(count)]


def shift(count, step):
    return [(i, (i + step) % count) for i in range(count)]


def after(x, *others):
    return lax.optimization_barrier((x,) + others)[0]


def gather_pipe(own, sections):
    half = own.shape[0] // 2
    up, down = shift(sections, 1), shift(sections, -1)
    low, high = own[:half], own[half:]
    before_low, behind_high = lax.ppermute(low, "pipe", up), lax.ppermute(high, "pipe", down)
    before_high, behind_low = lax.ppermute(high, "pipe", up), lax.ppermute(low, "pipe", down)
    far_low, far_high = lax.ppermute(before_low, "pipe", up), lax.ppermute(behind_high, "pipe", down)
    parts = [own, behind_low, behind_high, far_low, far_high, before_low, before_high]
    return jnp.concatenate(parts, axis=0)


def encode(stat):
    high = bf16(stat)
    rest = stat - f32(high)
    middle = bf16(rest)
    low = bf16(rest - f32(middle))
    row = lax.broadcasted_iota(jnp.int32, (SLAB, stat.shape[1]), 0)
    slab = jnp.where(row == 0, f32(high), jnp.where(row == 1, f32(middle), f32(low)))
    return bf16(jnp.where(row < 3, slab, 0.0))


def decode(slab):
    return jnp.sum(f32(slab), axis=0, keepdims=True)


def join_kernel(*refs):
    refs[-1][...] = jnp.zeros_like(refs[-1])


def join(*arrays):
    return pl.pallas_call(
        join_kernel,
        out_shape=pltpu.VMEM((8, 128), jnp.float32),
        in_specs=[ANY] * len(arrays),
        out_specs=VMEM,
        cost_estimate=COST,
    )(*arrays)


def collect_kernel(pieces, payloads, given, *refs):
    arrays = refs[:given]
    xs, squares, *packed = refs[len(refs) - 2 - len(payloads) :]
    if len(refs) > given + 2 + len(payloads):
        squares[...] = refs[given + 1][...]
    else:
        squares[...] = jnp.zeros_like(squares)
    for pack, out in zip(payloads, packed):
        row = 0
        for a, src, n in pack:
            out[row : row + n] = arrays[a][src : src + n]
            row += n
    blocks, rows, cols = xs.shape
    spans = squares.shape[0] // rows
    for a, src, n, span, k, dst in pieces:
        xs[span * (blocks // spans) + k, dst : dst + n] = arrays[a][src : src + n]
        for r in range(0, n, 128):
            at = span * rows + dst + r
            part = squares[at : at + 128]
            for c in range(0, cols, 128):
                x = f32(arrays[a][src + r : src + r + 128, c : c + 128])
                part = part + x * x
            squares[at : at + 128] = part


def collect(arrays, pieces, payloads, before, shape, total, cost):
    given = len(arrays)
    heights = [sum(n for _, _, n in pack) for pack in payloads]
    return pl.pallas_call(
        functools.partial(collect_kernel, pieces, payloads, given),
        out_shape=[
            pltpu.VMEM(shape, jnp.bfloat16),
            pltpu.VMEM((total, 128), jnp.float32),
            *[pltpu.VMEM((n, shape[2]), jnp.bfloat16) for n in heights],
        ],
        in_specs=[VMEM] * (given + len(before)),
        out_specs=[VMEM] * (2 + len(heights)),
        input_output_aliases={given: 0, given + 1: 1} if before else {},
        compiler_params=pltpu.CompilerParams(vmem_limit_bytes=16 * MIB),
        cost_estimate=cost,
    )(*arrays, *before)


def load_kernel(ids, weights, ws, token, sem):
    cols = ws.shape[1]
    copies = []
    for k in range(ws.shape[0]):
        at = pl.multiple_of(ids[k] * cols, cols)
        copies.append(pltpu.make_async_copy(weights.at[pl.ds(at, cols)], ws.at[k], sem.at[k]))
        copies[k].start()
    for copy in copies:
        copy.wait()
    token[...] = jnp.zeros_like(token)


def load(ids, weights):
    cols = weights.shape[1]
    count = weights.shape[0] // cols
    return pl.pallas_call(
        load_kernel,
        out_shape=[
            pltpu.VMEM((count, cols, cols), jnp.bfloat16),
            pltpu.VMEM((8, 128), jnp.float32),
        ],
        in_specs=[SMEM, HBM],
        out_specs=[VMEM, VMEM],
        scratch_shapes=[pltpu.SemaphoreType.DMA((count,))],
        compiler_params=pltpu.CompilerParams(vmem_limit_bytes=16 * MIB),
        cost_estimate=COST,
    )(ids, weights)


def forward_kernel(span, *refs):
    ids, okay, gain, query, cot, xs, squares, ws = refs[:8]
    if span > 0:
        attended_before, slab_before = refs[8:10]
    attended, grads, slab, inv, normed, acc = refs[-6:]
    rows, cols = acc.shape
    count = ws.shape[0]
    at = span * rows
    width = gain.shape[1]
    mean = jnp.sum(squares[at : at + rows], axis=1, keepdims=True) / width
    inv[...] = jnp.broadcast_to(lax.rsqrt(mean + epsilon), inv.shape)
    group = normed.shape[1] // cols
    for g in range(0, count, group):
        for i in range(group):
            k = g + i
            scaled = f32(xs[span * count + k]) * inv[:, :1]
            gain_row = gain[:, pl.ds(pl.multiple_of(ids[k] * cols, cols), cols)]
            normed[:, i * cols : (i + 1) * cols] = bf16(scaled * gain_row)
        block = ws[g : g + group].reshape(group * cols, cols)
        part = dot(normed[...], block, NN)
        acc[...] = part if g == 0 else acc[...] + part

    heads = cols // (2 * HS)
    scale = 1.0 / math.sqrt(HS)
    tokens = query.shape[0] // okay.shape[0]
    keep = okay[span].astype(jnp.float32)
    tok = span * tokens
    if span > 0:
        attended[:tok] = attended_before[...]
    for h in range(heads):
        lo, hi = h * HS, (heads + h) * HS
        key = bf16(acc[:, lo : lo + HS])
        value = bf16(acc[:, hi : hi + HS])
        q = query[tok : tok + tokens, lo : lo + HS]
        up = bf16(f32(cot[tok : tok + tokens, lo : lo + HS]) * keep)
        scores = dot(q, key, NT) * scale
        e = jnp.exp(scores - jnp.max(scores, axis=1, keepdims=True))
        prob = e / jnp.sum(e, axis=1, keepdims=True)
        low = bf16(prob)
        attended[tok : tok + tokens, lo : lo + HS] = bf16(dot(low, value, NN) * keep)
        prob_grad = dot(up, value, NT)
        inner = jnp.sum(prob_grad * prob, axis=1, keepdims=True)
        score_grad = bf16(prob * (prob_grad - inner) * scale)
        grads[:, lo : lo + HS] = bf16(dot(score_grad, q, TN))
        grads[:, hi : hi + HS] = bf16(dot(low, up, TN))
    stat = jnp.sum(f32(grads[...]) * acc[...], axis=1, keepdims=True)
    if span > 0:
        slab[:, :at] = slab_before[...]
    slab[:, at : at + rows] = encode(jnp.broadcast_to(stat, (rows, 128)).T[:1])


def forward(span, ids, okay, gain, query, cot, xs, squares, ws, *before):
    rows, cols = xs.shape[1:]
    tokens = query.shape[0] // okay.shape[0] * (span + 1)
    return pl.pallas_call(
        functools.partial(forward_kernel, span),
        out_shape=[
            pltpu.VMEM((tokens, query.shape[1]), jnp.bfloat16),
            pltpu.VMEM((rows, cols), jnp.bfloat16),
            pltpu.VMEM((SLAB, rows * (span + 1)), jnp.bfloat16),
            pltpu.VMEM((rows, 128), jnp.float32),
        ],
        in_specs=[SMEM, SMEM] + [VMEM] * (6 + len(before)),
        out_specs=[VMEM] * 4,
        scratch_shapes=[
            pltpu.VMEM((rows, GROUP * cols), jnp.bfloat16),
            pltpu.VMEM((rows, cols), jnp.float32),
        ],
        compiler_params=pltpu.CompilerParams(vmem_limit_bytes=16 * MIB),
        cost_estimate=COST if span == 0 else LIGHT,
    )(ids, okay, gain, query, cot, xs, squares, ws, *before)


def step_kernel(outs, spans, arrays, *refs):
    grads, weights, given, out_refs = refs[:spans], refs[spans], refs[spans + 1 :][:arrays], refs[spans + 1 + arrays :]
    for out, out_ref in zip(outs, out_refs):
        row = 0
        for s in out:
            if s[0] == "sum":
                _, span, first, n, k, adds = s
                total = dot(grads[span][first : first + n], weights[k], NT)
                for a, r in adds:
                    total = total + f32(given[a][r : r + n])
                out_ref[row : row + n] = total.astype(out_ref.dtype)
            elif s[0] == "copy":
                _, a, r, n = s
                out_ref[row : row + n] = given[a][r : r + n]
            else:
                _, (a, r), (b, t) = s
                n = SLAB
                pair = decode(given[a][r : r + n]) + decode(given[b][t : t + n])
                out_ref[row : row + n] = encode(pair)
            row += n


def step(grads, weights, outs, arrays, dtype, cost):
    cols = grads[0].shape[1]
    size = {"sum": lambda s: s[3], "copy": lambda s: s[3], "pair": lambda s: SLAB}
    heights = [sum(size[s[0]](s) for s in out) for out in outs]
    return pl.pallas_call(
        functools.partial(step_kernel, outs, len(grads), len(arrays)),
        out_shape=[pltpu.VMEM((n, cols), dtype) for n in heights],
        in_specs=[VMEM] * (len(grads) + 1 + len(arrays)),
        out_specs=[VMEM] * len(outs),
        compiler_params=pltpu.CompilerParams(vmem_limit_bytes=16 * MIB),
        cost_estimate=cost,
    )(*grads, weights, *arrays)


def tail_kernel(slabs, sections, width, *refs):
    ids, choose, gain, inv_a, inv_b, picked, before, swapped = refs[:8]
    a_up, a_down, b_up, b_down = refs[8:12]
    hops = refs[8:-6]
    share, far, ahead, behind, own, back = refs[-6:]
    rows, cols = back.shape
    half = rows // 2
    stat = jnp.zeros((1, rows), jnp.float32)
    for a, r in slabs:
        stat = stat + decode(hops[a][r : r + SLAB])
    mean = jnp.broadcast_to(stat / width, (128, rows)).T
    gain_row = gain[:, pl.ds(pl.multiple_of(ids[0] * cols, cols), cols)]
    sums = jnp.zeros((1, cols), jnp.float32)
    for c in range(0, rows, NL):
        if c < half:
            low, inv, up, down = c, inv_a, a_up, a_down
        else:
            low, inv, up, down = c - half, inv_b, b_up, b_down
        grads = before[c : c + NL] + f32(up[low : low + NL]) + f32(down[low : low + NL])
        if c < half:
            grads = grads + f32(swapped[c : c + NL])
        inverse = inv[low : low + NL, :1]
        scaled = f32(picked[c : c + NL]) * inverse
        sums = sums + jnp.sum(grads * scaled, axis=0, keepdims=True)
        back[c : c + NL] = inverse * (grads * gain_row - scaled * mean[c : c + NL, :1])
    share[...] = sums
    section = ids[ids.shape[0] - 1]
    for d, out in enumerate((own, ahead, far, behind)):
        for slot in range(NBR_DEV):
            n = lax.rem(section + d, sections) * NBR_DEV + slot
            part = jnp.zeros((NL, cols), jnp.float32)
            for k in range(rows // NL):
                part = part + jnp.where(choose[k] == n, back[k * NL : (k + 1) * NL], 0.0)
            out[slot * NL : (slot + 1) * NL] = part.astype(out.dtype)


def tail(ids, choose, gain, inv_a, inv_b, picked, before, swapped, hops, slabs, sections):
    rows, cols = before.shape
    block = (NBR_DEV * NL, cols)
    return pl.pallas_call(
        functools.partial(tail_kernel, slabs, sections, gain.size),
        out_shape=(
            pltpu.VMEM((1, cols), jnp.float32),
            pltpu.VMEM(block, jnp.bfloat16),
            pltpu.VMEM(block, jnp.float32),
            pltpu.VMEM(block, jnp.float32),
            pltpu.VMEM(block, jnp.float32),
        ),
        in_specs=[SMEM, SMEM] + [VMEM] * (6 + len(hops)),
        out_specs=(VMEM,) * 5,
        scratch_shapes=[pltpu.VMEM((rows, cols), jnp.float32)],
        compiler_params=pltpu.CompilerParams(vmem_limit_bytes=16 * MIB),
        cost_estimate=COST,
    )(ids, choose, gain, inv_a, inv_b, picked, before, swapped, *hops)


def local(queries, encoded_pool, choose, retrieval_ok, norm_gain, w_keyval, cotangent):
    count = lax.axis_size("tensor")
    sections = lax.axis_size("pipe")
    ring = count // Y
    reach = ring // 2
    place = lax.axis_index("tensor")
    section = lax.axis_index("pipe")
    cols = encoded_pool.shape[1]
    width = cols * count
    spans = retrieval_ok.shape[0]
    z_up, z_down, y_cross = z_shift(count, 1), z_shift(count, -1), y_swap(count)

    def send(x, perm):
        return lax.ppermute(x, "tensor", perm)

    order = jnp.arange(count + 1, dtype=jnp.int32)
    at_z = (place // Y + order // Y) % ring
    ids = jnp.where(order == count, section, at_z * Y + (place % Y + order) % Y)
    gain = norm_gain

    picks = choose.reshape(-1)
    spot = (picks // NBR_DEV - section + sections) % sections * NBR_DEV + picks % NBR_DEV
    pool_rows = gather_pipe(encoded_pool, sections)
    picked = pool_rows.reshape(-1, NL, cols)[spot].reshape(-1, cols)
    total = picked.shape[0]
    rows = total // spans

    half = rows // 2
    far = 2 * reach
    gathered = []

    def use(given, *payloads, gates=(), cost=COST):
        nonlocal gathered
        pieces = tuple((i, *piece) for i, (_, of_it) in enumerate(given) for piece in of_it)
        arrays = [array for array, _ in given]
        if gates:
            arrays[0] = after(arrays[0], *gates)
        *gathered, = collect(
            arrays, pieces, payloads, gathered, (spans * count, rows, cols), total, cost
        )
        packed = gathered[2:]
        gathered = gathered[:2]
        return [after(pack, gathered[1]) for pack in packed]

    def b_pieces(n, *ks):
        return [(i * n, n, 1, k, 0) for i, k in enumerate(ks)]

    def a_pieces(k):
        return [(0, rows, 0, k, 0), (rows, rows, 0, k + 1, 0)]

    first, second = picked[:rows], picked[rows:]
    b_low, b_high = send(second, z_up), send(second, z_down)
    partner, crossing = send(first, y_cross), send(second, y_cross)
    there = join(partner)
    a_low = a_high = after(jnp.concatenate([first, partner], axis=0), there)
    a_low, a_high = send(a_low, z_up), send(a_high, z_down)
    there = join(b_low, b_high, there)
    sent = after(jnp.concatenate([b_low, b_high], axis=0), there)
    near = [
        (first, [(0, rows, 0, 0, 0)]),
        (partner, [(0, rows, 0, 1, 0)]),
        (second, b_pieces(rows, 0)),
        (b_low, b_pieces(rows, 2 * (ring - 1))),
        (b_high, b_pieces(rows, 2)),
        (crossing, b_pieces(rows, 1)),
    ]
    b_low, b_high = send(after(b_low, there), z_up), send(after(b_high, there), z_down)
    crossing = send(sent, y_cross)
    weights = after(w_keyval, there)[0].reshape(width, -1)
    there = join(a_low, a_high, weights, there)
    near += [(a_low, a_pieces(2 * (ring - 1))), (a_high, a_pieces(2))]
    a_low, a_high = send(after(a_low, there), z_up), send(after(a_high, there), z_down)
    use(near, gates=(there,))
    w_here, token = load(ids, after(weights, gathered[1]))
    waiting = []
    for d in range(2, reach):
        low_k, high_k = 2 * (ring - d), 2 * d
        given = [(b_low, b_pieces(rows, low_k)), (b_high, b_pieces(rows, high_k))]
        payloads = [((0, 0, rows), (1, 0, rows))]
        if d == reach - 1:
            payloads += [((0, 0, half),), ((1, half, half),)]
        sent, *ends = use(given + waiting, *payloads, gates=(token,) if d == 2 else ())
        low, high = ends or (after(b_low, gathered[1]), after(b_high, gathered[1]))
        b_low, b_high = send(low, z_up), send(high, z_down)
        waiting = [(crossing, b_pieces(rows, low_k + 3, high_k - 1))]
        crossing = send(sent, y_cross)
        given = [(a_low, a_pieces(low_k)), (a_high, a_pieces(high_k))]
        payloads = [((0, 0, rows),), ((1, rows, rows),)] if d == reach - 1 else []
        ends = use(given, *payloads)
        low, high = ends or (after(a_low, gathered[1]), after(a_high, gathered[1]))
        a_low, a_high = send(low, z_up), send(high, z_down)
    (sent,) = use(
        [(b_low, [(0, half, 1, far, 0)]), (b_high, [(0, half, 1, far, half)])],
        ((0, 0, half), (1, 0, half)),
    )
    last = send(sent, y_cross)
    use([(a_low, [(0, rows, 0, far, 0)]), (a_high, [(0, rows, 0, far + 1, 0)])])

    inputs = (ids, retrieval_ok, gain, queries, cotangent)
    attended, grad_a, slab, inv_a = forward(0, *inputs, *gathered, w_here)

    last_step = [grad_a]

    def back(grads, outs, arrays, *gates, dtype=jnp.bfloat16, cost=COST):
        held = [after(grad, last_step[0], *gates) for grad in grads]
        got = step(held, w_here, outs, arrays, dtype, cost)
        last_step[0] = got[0]
        return got

    crossed = {}

    def cross(d, *gates):
        ks = [2 * d + 1] if d == 0 else [2 * d + 1, 2 * (ring - d) + 1]
        (got,) = back([grad_b], [[("sum", 0, 0, rows, k, []) for k in ks]], [], *gates)
        got = send(got, y_cross)
        for i, k in enumerate(ks):
            crossed[k - 1] = (got, i * rows)
        return got

    def a_step(d, a_up, a_down):
        if d == 0:
            outs = [[("sum", 0, 0, rows, 1, [(0, rows), (1, rows)])]]
            return send(back([grad_a], outs, [a_up, a_down])[0], y_cross)
        outs = []
        for arrived, k in ((0, 2 * d), (1, 2 * (ring - d))):
            own, other = [(arrived, 0)], [(arrived, rows)]
            if d == reach - 1:
                own, other = (own, []) if arrived == 0 else ([], [(1, 0)])
            outs.append([("sum", 0, 0, rows, k, own), ("sum", 0, 0, rows, k + 1, other)])
        a_up, a_down = back([grad_a], outs, [a_up, a_down])
        return send(a_up, z_up), send(a_down, z_down)

    a_up, a_down = back(
        [grad_a], [[("sum", 0, 0, rows, far, [])], [("sum", 0, 0, rows, far + 1, [])]], []
    )
    made = a_up
    a_up, a_down = send(a_up, z_up), send(a_down, z_down)
    use(
        waiting
        + [(crossing, b_pieces(rows, far + 3, far - 1)), (last, [(0, rows, 1, far + 1, 0)])],
        gates=(made,),
        cost=LIGHT,
    )
    attended, grad_b, slab, inv_b = forward(1, *inputs, *gathered, w_here, attended, slab)
    last_step = [grad_b]
    (c_far,) = back(
        [grad_b],
        [[("sum", 0, 0, rows, far + 1, []), ("copy", 0, 0, SLAB)]],
        [slab],
        cost=LIGHT,
    )
    c_far = send(c_far, y_cross)
    a_up, a_down = a_step(reach - 1, a_up, a_down)
    c_last = cross(reach - 1)
    pair = ("pair", (0, 0), (1, rows))
    b_up, b_down = back(
        [grad_b],
        [
            [("sum", 0, 0, half, far, [(1, 0)]), pair],
            [("sum", 0, half, half, far, [(1, half)]), pair],
        ],
        [slab, c_far],
    )
    hops, slabs = [b_up], [(0, half)]
    height = half
    b_up, b_down = send(b_up, z_up), send(b_down, z_down)
    for d in range(reach - 1, 0, -1):
        c_last = cross(d - 1, c_last)
        hops += [b_up, b_down]
        slabs += [(len(hops) - 2, height), (len(hops) - 1, height)]
        arrays = [b_up, b_down, crossed[2 * d][0], crossed[2 * (ring - d)][0]]
        outs = []
        for i, k in ((0, 2 * d), (1, 2 * (ring - d))):
            at = crossed[k][1]
            if d == reach - 1:
                low, high = [(2 + i, at)], [(2 + i, at + half)]
                (low if i == 0 else high).append((i, 0))
                out = [("sum", 0, 0, half, k, low), ("sum", 0, half, half, k, high)]
            else:
                out = [("sum", 0, 0, rows, k, [(i, 0), (2 + i, at)])]
            outs.append(out + [("copy", i, height, SLAB)])
        b_up, b_down = back([grad_b], outs, arrays)
        b_up, b_down = send(b_up, z_up), send(b_down, z_down)
        height = rows
        got = a_step(d - 1, a_up, a_down)
        if d > 1:
            a_up, a_down = got
    swapped = got
    (before,) = back(
        [grad_a, grad_b],
        [[("sum", 0, 0, rows, 0, []), ("sum", 1, 0, rows, 0, [(0, 0)])]],
        [crossed[0][0]],
        dtype=jnp.float32,
    )
    slabs = tuple((a + 4, r) for a, r in slabs) + ((3, rows),)
    share, far, ahead, behind, own = tail(
        ids, picks, gain, inv_a, inv_b, picked, before, swapped,
        [a_up, a_down, b_up, b_down] + hops, slabs, sections,
    )

    half = far.shape[0] // 2
    up = lax.ppermute(far[:half], "pipe", shift(sections, 1))
    down = lax.ppermute(far[half:], "pipe", shift(sections, -1))
    replicas = lax.axis_size("dp")
    share = share + lax.ppermute(share, "dp", [(i, i ^ 1) for i in range(replicas)])
    share = after(share, up)
    share = share + lax.ppermute(share, "dp", [(i, i ^ 2) for i in range(replicas)])
    ahead = jnp.concatenate([ahead[:half] + up, ahead[half:]], axis=0)
    behind = jnp.concatenate([behind[:half], behind[half:] + down], axis=0)
    up = lax.ppermute(bf16(ahead), "pipe", shift(sections, 1))
    down = lax.ppermute(bf16(behind), "pipe", shift(sections, -1))
    pool_grad = own + up + down
    return (attended, share, pool_grad)


def solution(mesh):
    return jax.shard_map(
        local,
        mesh=mesh,
        in_specs=(
            P(("pipe", "dp"), "tensor"),
            P(("pipe", "dp"), "tensor"),
            P(("pipe", "dp"), None),
            P(("pipe", "dp")),
            P("pipe", None),
            P("pipe", None, None, "tensor"),
            P(("pipe", "dp"), "tensor"),
        ),
        out_specs=(P(("pipe", "dp"), "tensor"), P("pipe", "tensor"), P(("pipe", "dp"), "tensor")),
        check_vma=False,
    )
```

```python
import functools
import math

import jax
import jax.numpy as jnp
from jax import lax
from jax.experimental import pallas as pl
from jax.experimental.pallas import tpu as pltpu
from jax.sharding import PartitionSpec as P

HS = 128
NL = 128
NBR_DEV = 2
Y = 2
SLAB = 16
GROUP = 4
MIB = 1 << 20

epsilon = 1e-05
VMEM = pl.BlockSpec(memory_space=pltpu.VMEM)
SMEM = pl.BlockSpec(memory_space=pltpu.SMEM)
HBM = pl.BlockSpec(memory_space=pltpu.HBM)
ANY = pl.BlockSpec(memory_space=pl.ANY)
COST = pl.CostEstimate(flops=4 * 10**9, bytes_accessed=1, transcendentals=0)
LIGHT = pl.CostEstimate(flops=1, bytes_accessed=1, transcendentals=0)
NT = (((1,), (1,)), ((), ()))
NN = (((1,), (0,)), ((), ()))
TN = (((0,), (0,)), ((), ()))


def bf16(x):
    return x.astype(jnp.bfloat16)


def f32(x):
    return x.astype(jnp.float32)


def dot(a, b, dims):
    return lax.dot_general(a, b, dims, preferred_element_type=jnp.float32)


def z_shift(count, step):
    ring = count // Y
    return [(i, ((i // Y + step) % ring) * Y + i % Y) for i in range(count)]


def y_swap(count):
    return [(i, i ^ 1) for i in range(count)]


def shift(count, step):
    return [(i, (i + step) % count) for i in range(count)]


def after(x, *others):
    return lax.optimization_barrier((x,) + others)[0]


def gather_pipe(own, sections):
    half = own.shape[0] // 2
    up, down = shift(sections, 1), shift(sections, -1)
    low, high = own[:half], own[half:]
    before_low, behind_high = lax.ppermute(low, "pipe", up), lax.ppermute(high, "pipe", down)
    before_high, behind_low = lax.ppermute(high, "pipe", up), lax.ppermute(low, "pipe", down)
    far_low, far_high = lax.ppermute(before_low, "pipe", up), lax.ppermute(behind_high, "pipe", down)
    parts = [own, behind_low, behind_high, far_low, far_high, before_low, before_high]
    return jnp.concatenate(parts, axis=0)


def encode(stat):
    high = bf16(stat)
    rest = stat - f32(high)
    middle = bf16(rest)
    low = bf16(rest - f32(middle))
    row = lax.broadcasted_iota(jnp.int32, (SLAB, stat.shape[1]), 0)
    slab = jnp.where(row == 0, f32(high), jnp.where(row == 1, f32(middle), f32(low)))
    return bf16(jnp.where(row < 3, slab, 0.0))


def decode(slab):
    return jnp.sum(f32(slab), axis=0, keepdims=True)


def join_kernel(*refs):
    refs[-1][...] = jnp.zeros_like(refs[-1])


def join(*arrays):
    return pl.pallas_call(
        join_kernel,
        out_shape=pltpu.VMEM((8, 128), jnp.float32),
        in_specs=[ANY] * len(arrays),
        out_specs=VMEM,
        cost_estimate=COST,
    )(*arrays)


def collect_kernel(pieces, payloads, given, *refs):
    arrays = refs[:given]
    xs, squares, *packed = refs[len(refs) - 2 - len(payloads) :]
    if len(refs) > given + 2 + len(payloads):
        squares[...] = refs[given + 1][...]
    else:
        squares[...] = jnp.zeros_like(squares)
    for pack, out in zip(payloads, packed):
        row = 0
        for a, src, n in pack:
            out[row : row + n] = arrays[a][src : src + n]
            row += n
    blocks, rows, cols = xs.shape
    spans = squares.shape[0] // rows
    for a, src, n, span, k, dst in pieces:
        xs[span * (blocks // spans) + k, dst : dst + n] = arrays[a][src : src + n]
        for r in range(0, n, 128):
            at = span * rows + dst + r
            part = squares[at : at + 128]
            for c in range(0, cols, 128):
                x = f32(arrays[a][src + r : src + r + 128, c : c + 128])
                part = part + x * x
            squares[at : at + 128] = part


def collect(arrays, pieces, payloads, before, shape, total, cost):
    given = len(arrays)
    heights = [sum(n for _, _, n in pack) for pack in payloads]
    return pl.pallas_call(
        functools.partial(collect_kernel, pieces, payloads, given),
        out_shape=[
            pltpu.VMEM(shape, jnp.bfloat16),
            pltpu.VMEM((total, 128), jnp.float32),
            *[pltpu.VMEM((n, shape[2]), jnp.bfloat16) for n in heights],
        ],
        in_specs=[VMEM] * (given + len(before)),
        out_specs=[VMEM] * (2 + len(heights)),
        input_output_aliases={given: 0, given + 1: 1} if before else {},
        compiler_params=pltpu.CompilerParams(vmem_limit_bytes=16 * MIB),
        cost_estimate=cost,
    )(*arrays, *before)


def load_kernel(ids, weights, ws, token, sem):
    cols = ws.shape[1]
    copies = []
    for k in range(ws.shape[0]):
        at = pl.multiple_of(ids[k] * cols, cols)
        copies.append(pltpu.make_async_copy(weights.at[pl.ds(at, cols)], ws.at[k], sem.at[k]))
        copies[k].start()
    for copy in copies:
        copy.wait()
    token[...] = jnp.zeros_like(token)


def load(ids, weights):
    cols = weights.shape[1]
    count = weights.shape[0] // cols
    return pl.pallas_call(
        load_kernel,
        out_shape=[
            pltpu.VMEM((count, cols, cols), jnp.bfloat16),
            pltpu.VMEM((8, 128), jnp.float32),
        ],
        in_specs=[SMEM, HBM],
        out_specs=[VMEM, VMEM],
        scratch_shapes=[pltpu.SemaphoreType.DMA((count,))],
        compiler_params=pltpu.CompilerParams(vmem_limit_bytes=16 * MIB),
        cost_estimate=COST,
    )(ids, weights)


def forward_kernel(span, *refs):
    ids, okay, gain, query, cot, xs, squares, ws = refs[:8]
    if span > 0:
        attended_before, slab_before = refs[8:10]
    attended, grads, slab, inv, normed, acc = refs[-6:]
    rows, cols = acc.shape
    count = ws.shape[0]
    at = span * rows
    width = gain.shape[1]
    mean = jnp.sum(squares[at : at + rows], axis=1, keepdims=True) / width
    inv[...] = jnp.broadcast_to(lax.rsqrt(mean + epsilon), inv.shape)
    group = normed.shape[1] // cols
    for g in range(0, count, group):
        for i in range(group):
            k = g + i
            scaled = f32(xs[span * count + k]) * inv[:, :1]
            gain_row = gain[:, pl.ds(pl.multiple_of(ids[k] * cols, cols), cols)]
            normed[:, i * cols : (i + 1) * cols] = bf16(scaled * gain_row)
        block = ws[g : g + group].reshape(group * cols, cols)
        part = dot(normed[...], block, NN)
        acc[...] = part if g == 0 else acc[...] + part

    heads = cols // (2 * HS)
    scale = 1.0 / math.sqrt(HS)
    tokens = query.shape[0] // okay.shape[0]
    keep = okay[span].astype(jnp.float32)
    tok = span * tokens
    if span > 0:
        attended[:tok] = attended_before[...]
    for h in range(heads):
        lo, hi = h * HS, (heads + h) * HS
        key = bf16(acc[:, lo : lo + HS])
        value = bf16(acc[:, hi : hi + HS])
        q = query[tok : tok + tokens, lo : lo + HS]
        up = bf16(f32(cot[tok : tok + tokens, lo : lo + HS]) * keep)
        scores = dot(q, key, NT) * scale
        e = jnp.exp(scores - jnp.max(scores, axis=1, keepdims=True))
        prob = e / jnp.sum(e, axis=1, keepdims=True)
        low = bf16(prob)
        attended[tok : tok + tokens, lo : lo + HS] = bf16(dot(low, value, NN) * keep)
        prob_grad = dot(up, value, NT)
        inner = jnp.sum(prob_grad * prob, axis=1, keepdims=True)
        score_grad = bf16(prob * (prob_grad - inner) * scale)
        grads[:, lo : lo + HS] = bf16(dot(score_grad, q, TN))
        grads[:, hi : hi + HS] = bf16(dot(low, up, TN))
    stat = jnp.sum(f32(grads[...]) * acc[...], axis=1, keepdims=True)
    if span > 0:
        slab[:, :at] = slab_before[...]
    slab[:, at : at + rows] = encode(jnp.broadcast_to(stat, (rows, 128)).T[:1])


def forward(span, ids, okay, gain, query, cot, xs, squares, ws, *before):
    rows, cols = xs.shape[1:]
    tokens = query.shape[0] // okay.shape[0] * (span + 1)
    return pl.pallas_call(
        functools.partial(forward_kernel, span),
        out_shape=[
            pltpu.VMEM((tokens, query.shape[1]), jnp.bfloat16),
            pltpu.VMEM((rows, cols), jnp.bfloat16),
            pltpu.VMEM((SLAB, rows * (span + 1)), jnp.bfloat16),
            pltpu.VMEM((rows, 128), jnp.float32),
        ],
        in_specs=[SMEM, SMEM] + [VMEM] * (6 + len(before)),
        out_specs=[VMEM] * 4,
        scratch_shapes=[
            pltpu.VMEM((rows, GROUP * cols), jnp.bfloat16),
            pltpu.VMEM((rows, cols), jnp.float32),
        ],
        compiler_params=pltpu.CompilerParams(vmem_limit_bytes=16 * MIB),
        cost_estimate=COST if span == 0 else LIGHT,
    )(ids, okay, gain, query, cot, xs, squares, ws, *before)


def step_kernel(outs, spans, arrays, *refs):
    grads, weights, given, out_refs = refs[:spans], refs[spans], refs[spans + 1 :][:arrays], refs[spans + 1 + arrays :]
    for out, out_ref in zip(outs, out_refs):
        row = 0
        for s in out:
            if s[0] == "sum":
                _, span, first, n, k, adds = s
                total = dot(grads[span][first : first + n], weights[k], NT)
                for a, r in adds:
                    total = total + f32(given[a][r : r + n])
                out_ref[row : row + n] = total.astype(out_ref.dtype)
            elif s[0] == "copy":
                _, a, r, n = s
                out_ref[row : row + n] = given[a][r : r + n]
            else:
                _, (a, r), (b, t) = s
                n = SLAB
                pair = decode(given[a][r : r + n]) + decode(given[b][t : t + n])
                out_ref[row : row + n] = encode(pair)
            row += n


def step(grads, weights, outs, arrays, dtype, cost):
    cols = grads[0].shape[1]
    size = {"sum": lambda s: s[3], "copy": lambda s: s[3], "pair": lambda s: SLAB}
    heights = [sum(size[s[0]](s) for s in out) for out in outs]
    return pl.pallas_call(
        functools.partial(step_kernel, outs, len(grads), len(arrays)),
        out_shape=[pltpu.VMEM((n, cols), dtype) for n in heights],
        in_specs=[VMEM] * (len(grads) + 1 + len(arrays)),
        out_specs=[VMEM] * len(outs),
        compiler_params=pltpu.CompilerParams(vmem_limit_bytes=16 * MIB),
        cost_estimate=cost,
    )(*grads, weights, *arrays)


def tail_kernel(slabs, sections, width, *refs):
    ids, choose, gain, inv_a, inv_b, picked, before, swapped = refs[:8]
    a_up, a_down, b_up, b_down = refs[8:12]
    hops = refs[8:-6]
    share, far, ahead, behind, own, back = refs[-6:]
    rows, cols = back.shape
    half = rows // 2
    stat = jnp.zeros((1, rows), jnp.float32)
    for a, r in slabs:
        stat = stat + decode(hops[a][r : r + SLAB])
    mean = jnp.broadcast_to(stat / width, (128, rows)).T
    gain_row = gain[:, pl.ds(pl.multiple_of(ids[0] * cols, cols), cols)]
    sums = jnp.zeros((1, cols), jnp.float32)
    for c in range(0, rows, NL):
        if c < half:
            low, inv, up, down = c, inv_a, a_up, a_down
        else:
            low, inv, up, down = c - half, inv_b, b_up, b_down
        grads = before[c : c + NL] + f32(up[low : low + NL]) + f32(down[low : low + NL])
        if c < half:
            grads = grads + f32(swapped[c : c + NL])
        inverse = inv[low : low + NL, :1]
        scaled = f32(picked[c : c + NL]) * inverse
        sums = sums + jnp.sum(grads * scaled, axis=0, keepdims=True)
        back[c : c + NL] = inverse * (grads * gain_row - scaled * mean[c : c + NL, :1])
    share[...] = sums
    section = ids[ids.shape[0] - 1]
    for d, out in enumerate((own, ahead, far, behind)):
        for slot in range(NBR_DEV):
            n = lax.rem(section + d, sections) * NBR_DEV + slot
            part = jnp.zeros((NL, cols), jnp.float32)
            for k in range(rows // NL):
                part = part + jnp.where(choose[k // 2, k % 2] == n, back[k * NL : (k + 1) * NL], 0.0)
            out[slot * NL : (slot + 1) * NL] = part.astype(out.dtype)


def tail(ids, choose, gain, inv_a, inv_b, picked, before, swapped, hops, slabs, sections):
    rows, cols = before.shape
    block = (NBR_DEV * NL, cols)
    return pl.pallas_call(
        functools.partial(tail_kernel, slabs, sections, gain.size),
        out_shape=(
            pltpu.VMEM((1, cols), jnp.float32),
            pltpu.VMEM(block, jnp.bfloat16),
            pltpu.VMEM(block, jnp.float32),
            pltpu.VMEM(block, jnp.float32),
            pltpu.VMEM(block, jnp.float32),
        ),
        in_specs=[SMEM, SMEM] + [VMEM] * (6 + len(hops)),
        out_specs=(VMEM,) * 5,
        scratch_shapes=[pltpu.VMEM((rows, cols), jnp.float32)],
        compiler_params=pltpu.CompilerParams(vmem_limit_bytes=16 * MIB),
        cost_estimate=LIGHT,
    )(ids, choose, gain, inv_a, inv_b, picked, before, swapped, *hops)


def local(queries, encoded_pool, choose, retrieval_ok, norm_gain, w_keyval, cotangent):
    count = lax.axis_size("tensor")
    sections = lax.axis_size("pipe")
    ring = count // Y
    reach = ring // 2
    place = lax.axis_index("tensor")
    section = lax.axis_index("pipe")
    cols = encoded_pool.shape[1]
    width = cols * count
    spans = retrieval_ok.shape[0]
    z_up, z_down, y_cross = z_shift(count, 1), z_shift(count, -1), y_swap(count)

    def send(x, perm):
        return lax.ppermute(x, "tensor", perm)

    order = jnp.arange(count + 1, dtype=jnp.int32)
    at_z = (place // Y + order // Y) % ring
    ids = jnp.where(order == count, section, at_z * Y + (place % Y + order) % Y)
    gain = norm_gain

    picks = choose.reshape(-1)
    spot = (picks // NBR_DEV - section + sections) % sections * NBR_DEV + picks % NBR_DEV
    pool_rows = gather_pipe(encoded_pool, sections)
    picked = pool_rows.reshape(-1, NL, cols)[spot].reshape(-1, cols)
    total = picked.shape[0]
    rows = total // spans

    half = rows // 2
    far = 2 * reach
    gathered = []

    def use(given, *payloads, gates=(), cost=COST):
        nonlocal gathered
        pieces = tuple((i, *piece) for i, (_, of_it) in enumerate(given) for piece in of_it)
        arrays = [array for array, _ in given]
        if gates:
            arrays[0] = after(arrays[0], *gates)
        *gathered, = collect(
            arrays, pieces, payloads, gathered, (spans * count, rows, cols), total, cost
        )
        packed = gathered[2:]
        gathered = gathered[:2]
        return [after(pack, gathered[1]) for pack in packed]

    def b_pieces(n, *ks):
        return [(i * n, n, 1, k, 0) for i, k in enumerate(ks)]

    def a_pieces(k):
        return [(0, rows, 0, k, 0), (rows, rows, 0, k + 1, 0)]

    first, second = picked[:rows], picked[rows:]
    b_low, b_high = send(second, z_up), send(second, z_down)
    partner, crossing = send(first, y_cross), send(second, y_cross)
    there = join(partner)
    a_low = a_high = after(jnp.concatenate([first, partner], axis=0), there)
    a_low, a_high = send(a_low, z_up), send(a_high, z_down)
    there = join(b_low, b_high, there)
    sent = after(jnp.concatenate([b_low, b_high], axis=0), there)
    near = [
        (first, [(0, rows, 0, 0, 0)]),
        (partner, [(0, rows, 0, 1, 0)]),
        (second, b_pieces(rows, 0)),
        (b_low, b_pieces(rows, 2 * (ring - 1))),
        (b_high, b_pieces(rows, 2)),
        (crossing, b_pieces(rows, 1)),
    ]
    b_low, b_high = send(after(b_low, there), z_up), send(after(b_high, there), z_down)
    crossing = send(sent, y_cross)
    weights = after(w_keyval, there)[0].reshape(width, -1)
    there = join(a_low, a_high, weights, there)
    near += [(a_low, a_pieces(2 * (ring - 1))), (a_high, a_pieces(2))]
    a_low, a_high = send(after(a_low, there), z_up), send(after(a_high, there), z_down)
    use(near, gates=(there,))
    w_here, token = load(ids, after(weights, gathered[1]))
    waiting = []
    for d in range(2, reach):
        low_k, high_k = 2 * (ring - d), 2 * d
        given = [(b_low, b_pieces(rows, low_k)), (b_high, b_pieces(rows, high_k))]
        payloads = [((0, 0, rows), (1, 0, rows))]
        if d == reach - 1:
            payloads += [((0, 0, half),), ((1, half, half),)]
        sent, *ends = use(given + waiting, *payloads, gates=(token,) if d == 2 else ())
        low, high = ends or (after(b_low, gathered[1]), after(b_high, gathered[1]))
        b_low, b_high = send(low, z_up), send(high, z_down)
        waiting = [(crossing, b_pieces(rows, low_k + 3, high_k - 1))]
        crossing = send(sent, y_cross)
        given = [(a_low, a_pieces(low_k)), (a_high, a_pieces(high_k))]
        payloads = [((0, 0, rows),), ((1, rows, rows),)] if d == reach - 1 else []
        ends = use(given, *payloads)
        low, high = ends or (after(a_low, gathered[1]), after(a_high, gathered[1]))
        a_low, a_high = send(low, z_up), send(high, z_down)
    (sent,) = use(
        [(b_low, [(0, half, 1, far, 0)]), (b_high, [(0, half, 1, far, half)])],
        ((0, 0, half), (1, 0, half)),
    )
    last = send(sent, y_cross)
    use([(a_low, [(0, rows, 0, far, 0)]), (a_high, [(0, rows, 0, far + 1, 0)])])

    inputs = (ids, retrieval_ok, gain, queries, cotangent)
    attended, grad_a, slab, inv_a = forward(0, *inputs, *gathered, w_here)

    last_step = [grad_a]

    def back(grads, outs, arrays, *gates, dtype=jnp.bfloat16, cost=COST):
        held = [after(grad, last_step[0], *gates) for grad in grads]
        got = step(held, w_here, outs, arrays, dtype, cost)
        last_step[0] = got[0]
        return got

    crossed = {}

    def cross(d, *gates):
        ks = [2 * d + 1] if d == 0 else [2 * d + 1, 2 * (ring - d) + 1]
        (got,) = back([grad_b], [[("sum", 0, 0, rows, k, []) for k in ks]], [], *gates)
        got = send(got, y_cross)
        for i, k in enumerate(ks):
            crossed[k - 1] = (got, i * rows)
        return got

    def a_step(d, a_up, a_down):
        outs = []
        for arrived, k in ((0, 2 * d), (1, 2 * (ring - d))):
            own, other = [(arrived, 0)], [(arrived, rows)]
            if d == reach - 1:
                own, other = (own, []) if arrived == 0 else ([], [(1, 0)])
            outs.append([("sum", 0, 0, rows, k, own), ("sum", 0, 0, rows, k + 1, other)])
        if d > 1:
            a_up, a_down = back([grad_a], outs, [a_up, a_down])
            return send(a_up, z_up), send(a_down, z_down)
        parts = [[out[i]] for i in (1, 0) for out in outs]
        other_up, other_down, a_up, a_down = back([grad_a], parts, [a_up, a_down])
        other_up, other_down = send(other_up, z_up), send(other_down, z_down)
        a_up, a_down = send(a_up, z_up), send(a_down, z_down)
        return a_up, a_down, other_up, other_down

    def a_end(other_up, other_down):
        outs = [[("sum", 0, 0, rows, 1, [(0, 0), (1, 0)])]]
        return send(back([grad_a], outs, [other_up, other_down], cost=LIGHT)[0], y_cross)

    a_up, a_down = back(
        [grad_a], [[("sum", 0, 0, rows, far, [])], [("sum", 0, 0, rows, far + 1, [])]], []
    )
    made = a_up
    a_up, a_down = send(a_up, z_up), send(a_down, z_down)
    use(
        waiting
        + [(crossing, b_pieces(rows, far + 3, far - 1)), (last, [(0, rows, 1, far + 1, 0)])],
        gates=(made,),
        cost=LIGHT,
    )
    attended, grad_b, slab, inv_b = forward(1, *inputs, *gathered, w_here, attended, slab)
    last_step = [grad_b]
    (c_far,) = back(
        [grad_b],
        [[("sum", 0, 0, rows, far + 1, []), ("copy", 0, 0, SLAB)]],
        [slab],
        cost=LIGHT,
    )
    c_far = send(c_far, y_cross)
    a_up, a_down = a_step(reach - 1, a_up, a_down)
    c_last = cross(reach - 1)
    pair = ("pair", (0, 0), (1, rows))
    b_up, b_down = back(
        [grad_b],
        [
            [("sum", 0, 0, half, far, [(1, 0)]), pair],
            [("sum", 0, half, half, far, [(1, half)]), pair],
        ],
        [slab, c_far],
    )
    hops, slabs = [b_up], [(0, half)]
    height = half
    b_up, b_down = send(b_up, z_up), send(b_down, z_down)
    for d in range(reach - 1, 0, -1):
        c_last = cross(d - 1, c_last)
        hops += [b_up, b_down]
        slabs += [(len(hops) - 2, height), (len(hops) - 1, height)]
        arrays = [b_up, b_down, crossed[2 * d][0], crossed[2 * (ring - d)][0]]
        outs = []
        for i, k in ((0, 2 * d), (1, 2 * (ring - d))):
            at = crossed[k][1]
            if d == reach - 1:
                low, high = [(2 + i, at)], [(2 + i, at + half)]
                (low if i == 0 else high).append((i, 0))
                out = [("sum", 0, 0, half, k, low), ("sum", 0, half, half, k, high)]
            else:
                out = [("sum", 0, 0, rows, k, [(i, 0), (2 + i, at)])]
            outs.append(out + [("copy", i, height, SLAB)])
        b_up, b_down = back([grad_b], outs, arrays)
        b_up, b_down = send(b_up, z_up), send(b_down, z_down)
        height = rows
        if d > 1:
            a_up, a_down, *others = a_step(d - 1, a_up, a_down)
    swapped = a_end(*others)
    (before,) = back(
        [grad_a, grad_b],
        [[("sum", 0, 0, rows, 0, []), ("sum", 1, 0, rows, 0, [(0, 0)])]],
        [crossed[0][0]],
        dtype=jnp.float32,
        cost=LIGHT,
    )
    slabs = tuple((a + 4, r) for a, r in slabs) + ((3, rows),)
    share, far, ahead, behind, own = tail(
        ids, choose, gain, inv_a, inv_b, picked, before, swapped,
        [a_up, a_down, b_up, b_down] + hops, slabs, sections,
    )

    half = far.shape[0] // 2
    up = lax.ppermute(far[:half], "pipe", shift(sections, 1))
    down = lax.ppermute(far[half:], "pipe", shift(sections, -1))
    replicas = lax.axis_size("dp")
    share = share + lax.ppermute(share, "dp", [(i, i ^ 1) for i in range(replicas)])
    share = after(share, up)
    share = share + lax.ppermute(share, "dp", [(i, i ^ 2) for i in range(replicas)])
    ahead = jnp.concatenate([ahead[:half] + up, ahead[half:]], axis=0)
    behind = jnp.concatenate([behind[:half], behind[half:] + down], axis=0)
    up = lax.ppermute(bf16(ahead), "pipe", shift(sections, 1))
    down = lax.ppermute(bf16(behind), "pipe", shift(sections, -1))
    pool_grad = own + up + down
    return (attended, share, pool_grad)


def solution(mesh):
    return jax.shard_map(
        local,
        mesh=mesh,
        in_specs=(
            P(("pipe", "dp"), "tensor"),
            P(("pipe", "dp"), "tensor"),
            P(("pipe", "dp"), None),
            P(("pipe", "dp")),
            P("pipe", None),
            P("pipe", None, None, "tensor"),
            P(("pipe", "dp"), "tensor"),
        ),
        out_specs=(P(("pipe", "dp"), "tensor"), P("pipe", "tensor"), P(("pipe", "dp"), "tensor")),
        check_vma=False,
    )
```

```python
import functools
import math

import jax
import jax.numpy as jnp
from jax import lax
from jax.experimental import pallas as pl
from jax.experimental.pallas import tpu as pltpu
from jax.sharding import PartitionSpec as P

HS = 128
NL = 128
NBR_DEV = 2
Y = 2
SLAB = 16
GROUP = 4
MIB = 1 << 20

epsilon = 1e-05
VMEM = pl.BlockSpec(memory_space=pltpu.VMEM)
SMEM = pl.BlockSpec(memory_space=pltpu.SMEM)
HBM = pl.BlockSpec(memory_space=pltpu.HBM)
ANY = pl.BlockSpec(memory_space=pl.ANY)
COST = pl.CostEstimate(flops=3 * 10**9, bytes_accessed=1, transcendentals=0)
LIGHT = pl.CostEstimate(flops=1, bytes_accessed=1, transcendentals=0)
NT = (((1,), (1,)), ((), ()))
NN = (((1,), (0,)), ((), ()))
TN = (((0,), (0,)), ((), ()))


def bf16(x):
    return x.astype(jnp.bfloat16)


def f32(x):
    return x.astype(jnp.float32)


def dot(a, b, dims):
    return lax.dot_general(a, b, dims, preferred_element_type=jnp.float32)


def z_shift(count, step):
    ring = count // Y
    return [(i, ((i // Y + step) % ring) * Y + i % Y) for i in range(count)]


def y_swap(count):
    return [(i, i ^ 1) for i in range(count)]


def shift(count, step):
    return [(i, (i + step) % count) for i in range(count)]


def after(x, *others):
    return lax.optimization_barrier((x,) + others)[0]


def gather_pipe(own, sections):
    half = own.shape[0] // 2
    up, down = shift(sections, 1), shift(sections, -1)
    low, high = own[:half], own[half:]
    before_low, behind_high = lax.ppermute(low, "pipe", up), lax.ppermute(high, "pipe", down)
    before_high, behind_low = lax.ppermute(high, "pipe", up), lax.ppermute(low, "pipe", down)
    far_low, far_high = lax.ppermute(before_low, "pipe", up), lax.ppermute(behind_high, "pipe", down)
    parts = [own, behind_low, behind_high, far_low, far_high, before_low, before_high]
    return jnp.concatenate(parts, axis=0)


def encode(stat):
    high = bf16(stat)
    rest = stat - f32(high)
    middle = bf16(rest)
    low = bf16(rest - f32(middle))
    row = lax.broadcasted_iota(jnp.int32, (SLAB, stat.shape[1]), 0)
    slab = jnp.where(row == 0, f32(high), jnp.where(row == 1, f32(middle), f32(low)))
    return bf16(jnp.where(row < 3, slab, 0.0))


def decode(slab):
    return jnp.sum(f32(slab), axis=0, keepdims=True)


def join_kernel(*refs):
    refs[-1][...] = jnp.zeros_like(refs[-1])


def join(*arrays):
    return pl.pallas_call(
        join_kernel,
        out_shape=pltpu.VMEM((8, 128), jnp.float32),
        in_specs=[ANY] * len(arrays),
        out_specs=VMEM,
        cost_estimate=COST,
    )(*arrays)


def collect_kernel(pieces, payloads, given, *refs):
    arrays = refs[:given]
    xs, squares, *packed = refs[len(refs) - 2 - len(payloads) :]
    if len(refs) > given + 2 + len(payloads):
        squares[...] = refs[given + 1][...]
    else:
        squares[...] = jnp.zeros_like(squares)
    for pack, out in zip(payloads, packed):
        row = 0
        for a, src, n in pack:
            out[row : row + n] = arrays[a][src : src + n]
            row += n
    blocks, rows, cols = xs.shape
    spans = squares.shape[0] // rows
    for a, src, n, span, k, dst in pieces:
        xs[span * (blocks // spans) + k, dst : dst + n] = arrays[a][src : src + n]
        for r in range(0, n, 128):
            at = span * rows + dst + r
            part = squares[at : at + 128]
            for c in range(0, cols, 128):
                x = f32(arrays[a][src + r : src + r + 128, c : c + 128])
                part = part + x * x
            squares[at : at + 128] = part


def collect(arrays, pieces, payloads, before, shape, total, cost):
    given = len(arrays)
    heights = [sum(n for _, _, n in pack) for pack in payloads]
    return pl.pallas_call(
        functools.partial(collect_kernel, pieces, payloads, given),
        out_shape=[
            pltpu.VMEM(shape, jnp.bfloat16),
            pltpu.VMEM((total, 128), jnp.float32),
            *[pltpu.VMEM((n, shape[2]), jnp.bfloat16) for n in heights],
        ],
        in_specs=[VMEM] * (given + len(before)),
        out_specs=[VMEM] * (2 + len(heights)),
        input_output_aliases={given: 0, given + 1: 1} if before else {},
        compiler_params=pltpu.CompilerParams(vmem_limit_bytes=16 * MIB),
        cost_estimate=cost,
    )(*arrays, *before)


def load_kernel(ids, weights, ws, token, sem):
    cols = ws.shape[1]
    copies = []
    for k in range(ws.shape[0]):
        at = pl.multiple_of(ids[k] * cols, cols)
        copies.append(pltpu.make_async_copy(weights.at[pl.ds(at, cols)], ws.at[k], sem.at[k]))
        copies[k].start()
    for copy in copies:
        copy.wait()
    token[...] = jnp.zeros_like(token)


def load(ids, weights):
    cols = weights.shape[1]
    count = weights.shape[0] // cols
    return pl.pallas_call(
        load_kernel,
        out_shape=[
            pltpu.VMEM((count, cols, cols), jnp.bfloat16),
            pltpu.VMEM((8, 128), jnp.float32),
        ],
        in_specs=[SMEM, HBM],
        out_specs=[VMEM, VMEM],
        scratch_shapes=[pltpu.SemaphoreType.DMA((count,))],
        compiler_params=pltpu.CompilerParams(vmem_limit_bytes=16 * MIB),
        cost_estimate=COST,
    )(ids, weights)


def forward_kernel(span, *refs):
    ids, okay, gain, query, cot, xs, squares, ws = refs[:8]
    if span > 0:
        attended_before, slab_before = refs[8:10]
    attended, grads, slab, inv, normed, acc = refs[-6:]
    rows, cols = acc.shape
    count = ws.shape[0]
    at = span * rows
    width = gain.shape[1]
    mean = jnp.sum(squares[at : at + rows], axis=1, keepdims=True) / width
    inv[...] = jnp.broadcast_to(lax.rsqrt(mean + epsilon), inv.shape)
    group = normed.shape[1] // cols
    for g in range(0, count, group):
        for i in range(group):
            k = g + i
            scaled = f32(xs[span * count + k]) * inv[:, :1]
            gain_row = gain[:, pl.ds(pl.multiple_of(ids[k] * cols, cols), cols)]
            normed[:, i * cols : (i + 1) * cols] = bf16(scaled * gain_row)
        block = ws[g : g + group].reshape(group * cols, cols)
        part = dot(normed[...], block, NN)
        acc[...] = part if g == 0 else acc[...] + part

    heads = cols // (2 * HS)
    scale = 1.0 / math.sqrt(HS)
    tokens = query.shape[0] // okay.shape[0]
    keep = okay[span].astype(jnp.float32)
    tok = span * tokens
    if span > 0:
        attended[:tok] = attended_before[...]
    for h in range(heads):
        lo, hi = h * HS, (heads + h) * HS
        key = bf16(acc[:, lo : lo + HS])
        value = bf16(acc[:, hi : hi + HS])
        q = query[tok : tok + tokens, lo : lo + HS]
        up = bf16(f32(cot[tok : tok + tokens, lo : lo + HS]) * keep)
        scores = dot(q, key, NT) * scale
        e = jnp.exp(scores - jnp.max(scores, axis=1, keepdims=True))
        prob = e / jnp.sum(e, axis=1, keepdims=True)
        low = bf16(prob)
        attended[tok : tok + tokens, lo : lo + HS] = bf16(dot(low, value, NN) * keep)
        prob_grad = dot(up, value, NT)
        inner = jnp.sum(prob_grad * prob, axis=1, keepdims=True)
        score_grad = bf16(prob * (prob_grad - inner) * scale)
        grads[:, lo : lo + HS] = bf16(dot(score_grad, q, TN))
        grads[:, hi : hi + HS] = bf16(dot(low, up, TN))
    stat = jnp.sum(f32(grads[...]) * acc[...], axis=1, keepdims=True)
    if span > 0:
        slab[:, :at] = slab_before[...]
    slab[:, at : at + rows] = encode(jnp.broadcast_to(stat, (rows, 128)).T[:1])


def forward(span, ids, okay, gain, query, cot, xs, squares, ws, *before):
    rows, cols = xs.shape[1:]
    tokens = query.shape[0] // okay.shape[0] * (span + 1)
    return pl.pallas_call(
        functools.partial(forward_kernel, span),
        out_shape=[
            pltpu.VMEM((tokens, query.shape[1]), jnp.bfloat16),
            pltpu.VMEM((rows, cols), jnp.bfloat16),
            pltpu.VMEM((SLAB, rows * (span + 1)), jnp.bfloat16),
            pltpu.VMEM((rows, 128), jnp.float32),
        ],
        in_specs=[SMEM, SMEM] + [VMEM] * (6 + len(before)),
        out_specs=[VMEM] * 4,
        scratch_shapes=[
            pltpu.VMEM((rows, GROUP * cols), jnp.bfloat16),
            pltpu.VMEM((rows, cols), jnp.float32),
        ],
        compiler_params=pltpu.CompilerParams(vmem_limit_bytes=16 * MIB),
        cost_estimate=COST if span == 0 else LIGHT,
    )(ids, okay, gain, query, cot, xs, squares, ws, *before)


def step_kernel(outs, spans, arrays, *refs):
    grads, weights, given, out_refs = refs[:spans], refs[spans], refs[spans + 1 :][:arrays], refs[spans + 1 + arrays :]
    for out, out_ref in zip(outs, out_refs):
        row = 0
        for s in out:
            if s[0] == "sum":
                _, span, first, n, k, adds = s
                total = dot(grads[span][first : first + n], weights[k], NT)
                for a, r in adds:
                    total = total + f32(given[a][r : r + n])
                out_ref[row : row + n] = total.astype(out_ref.dtype)
            elif s[0] == "copy":
                _, a, r, n = s
                out_ref[row : row + n] = given[a][r : r + n]
            else:
                _, (a, r), (b, t) = s
                n = SLAB
                pair = decode(given[a][r : r + n]) + decode(given[b][t : t + n])
                out_ref[row : row + n] = encode(pair)
            row += n


def step(grads, weights, outs, arrays, dtype, cost):
    cols = grads[0].shape[1]
    size = {"sum": lambda s: s[3], "copy": lambda s: s[3], "pair": lambda s: SLAB}
    heights = [sum(size[s[0]](s) for s in out) for out in outs]
    return pl.pallas_call(
        functools.partial(step_kernel, outs, len(grads), len(arrays)),
        out_shape=[pltpu.VMEM((n, cols), dtype) for n in heights],
        in_specs=[VMEM] * (len(grads) + 1 + len(arrays)),
        out_specs=[VMEM] * len(outs),
        compiler_params=pltpu.CompilerParams(vmem_limit_bytes=16 * MIB),
        cost_estimate=cost,
    )(*grads, weights, *arrays)


def tail_kernel(slabs, sections, width, *refs):
    ids, choose, gain, inv_a, inv_b, picked, before, swapped = refs[:8]
    a_up, a_down, b_up, b_down = refs[8:12]
    hops = refs[8:-6]
    share, far, ahead, behind, own, back = refs[-6:]
    rows, cols = back.shape
    half = rows // 2
    stat = jnp.zeros((1, rows), jnp.float32)
    for a, r in slabs:
        stat = stat + decode(hops[a][r : r + SLAB])
    mean = jnp.broadcast_to(stat / width, (128, rows)).T
    gain_row = gain[:, pl.ds(pl.multiple_of(ids[0] * cols, cols), cols)]
    sums = jnp.zeros((1, cols), jnp.float32)
    for c in range(0, rows, NL):
        if c < half:
            low, inv, up, down = c, inv_a, a_up, a_down
        else:
            low, inv, up, down = c - half, inv_b, b_up, b_down
        grads = before[c : c + NL] + f32(up[low : low + NL]) + f32(down[low : low + NL])
        if c < half:
            grads = grads + f32(swapped[c : c + NL])
        inverse = inv[low : low + NL, :1]
        scaled = f32(picked[c : c + NL]) * inverse
        sums = sums + jnp.sum(grads * scaled, axis=0, keepdims=True)
        back[c : c + NL] = inverse * (grads * gain_row - scaled * mean[c : c + NL, :1])
    share[...] = sums
    section = ids[ids.shape[0] - 1]
    for d, out in enumerate((own, ahead, far, behind)):
        for slot in range(NBR_DEV):
            n = lax.rem(section + d, sections) * NBR_DEV + slot
            part = jnp.zeros((NL, cols), jnp.float32)
            for k in range(rows // NL):
                part = part + jnp.where(choose[k // 2, k % 2] == n, back[k * NL : (k + 1) * NL], 0.0)
            out[slot * NL : (slot + 1) * NL] = part.astype(out.dtype)


def tail(ids, choose, gain, inv_a, inv_b, picked, before, swapped, hops, slabs, sections):
    rows, cols = before.shape
    block = (NBR_DEV * NL, cols)
    return pl.pallas_call(
        functools.partial(tail_kernel, slabs, sections, gain.size),
        out_shape=(
            pltpu.VMEM((1, cols), jnp.float32),
            pltpu.VMEM(block, jnp.bfloat16),
            pltpu.VMEM(block, jnp.float32),
            pltpu.VMEM(block, jnp.float32),
            pltpu.VMEM(block, jnp.float32),
        ),
        in_specs=[SMEM, SMEM] + [VMEM] * (6 + len(hops)),
        out_specs=(VMEM,) * 5,
        scratch_shapes=[pltpu.VMEM((rows, cols), jnp.float32)],
        compiler_params=pltpu.CompilerParams(vmem_limit_bytes=16 * MIB),
        cost_estimate=LIGHT,
    )(ids, choose, gain, inv_a, inv_b, picked, before, swapped, *hops)


def local(queries, encoded_pool, choose, retrieval_ok, norm_gain, w_keyval, cotangent):
    count = lax.axis_size("tensor")
    sections = lax.axis_size("pipe")
    ring = count // Y
    reach = ring // 2
    place = lax.axis_index("tensor")
    section = lax.axis_index("pipe")
    cols = encoded_pool.shape[1]
    width = cols * count
    spans = retrieval_ok.shape[0]
    z_up, z_down, y_cross = z_shift(count, 1), z_shift(count, -1), y_swap(count)

    def send(x, perm):
        return lax.ppermute(x, "tensor", perm)

    order = jnp.arange(count + 1, dtype=jnp.int32)
    at_z = (place // Y + order // Y) % ring
    ids = jnp.where(order == count, section, at_z * Y + (place % Y + order) % Y)
    gain = norm_gain

    picks = choose.reshape(-1)
    spot = (picks // NBR_DEV - section + sections) % sections * NBR_DEV + picks % NBR_DEV
    pool_rows = gather_pipe(encoded_pool, sections)
    picked = pool_rows.reshape(-1, NL, cols)[spot].reshape(-1, cols)
    total = picked.shape[0]
    rows = total // spans

    half = rows // 2
    far = 2 * reach
    gathered = []

    def use(given, *payloads, gates=(), cost=COST):
        nonlocal gathered
        pieces = tuple((i, *piece) for i, (_, of_it) in enumerate(given) for piece in of_it)
        arrays = [array for array, _ in given]
        if gates:
            arrays[0] = after(arrays[0], *gates)
        *gathered, = collect(
            arrays, pieces, payloads, gathered, (spans * count, rows, cols), total, cost
        )
        packed = gathered[2:]
        gathered = gathered[:2]
        return [after(pack, gathered[1]) for pack in packed]

    def b_pieces(n, *ks):
        return [(i * n, n, 1, k, 0) for i, k in enumerate(ks)]

    def a_pieces(k):
        return [(0, rows, 0, k, 0), (rows, rows, 0, k + 1, 0)]

    first, second = picked[:rows], picked[rows:]
    b_low, b_high = send(second, z_up), send(second, z_down)
    partner, crossing = send(first, y_cross), send(second, y_cross)
    there = join(partner)
    a_low = a_high = after(jnp.concatenate([first, partner], axis=0), there)
    a_low, a_high = send(a_low, z_up), send(a_high, z_down)
    there = join(b_low, b_high, there)
    sent = after(jnp.concatenate([b_low, b_high], axis=0), there)
    near = [
        (first, [(0, rows, 0, 0, 0)]),
        (partner, [(0, rows, 0, 1, 0)]),
        (second, b_pieces(rows, 0)),
        (b_low, b_pieces(rows, 2 * (ring - 1))),
        (b_high, b_pieces(rows, 2)),
        (crossing, b_pieces(rows, 1)),
    ]
    b_low, b_high = send(after(b_low, there), z_up), send(after(b_high, there), z_down)
    crossing = send(sent, y_cross)
    weights = after(w_keyval, there)[0].reshape(width, -1)
    there = join(a_low, a_high, weights, there)
    near += [(a_low, a_pieces(2 * (ring - 1))), (a_high, a_pieces(2))]
    a_low, a_high = send(after(a_low, there), z_up), send(after(a_high, there), z_down)
    use(near, gates=(there,))
    w_here, token = load(ids, after(weights, gathered[1]))
    waiting = []
    for d in range(2, reach):
        low_k, high_k = 2 * (ring - d), 2 * d
        given = [(b_low, b_pieces(rows, low_k)), (b_high, b_pieces(rows, high_k))]
        payloads = [((0, 0, rows), (1, 0, rows))]
        if d == reach - 1:
            payloads += [((0, 0, half),), ((1, half, half),)]
        sent, *ends = use(given + waiting, *payloads, gates=(token,) if d == 2 else ())
        low, high = ends or (after(b_low, gathered[1]), after(b_high, gathered[1]))
        b_low, b_high = send(low, z_up), send(high, z_down)
        waiting = [(crossing, b_pieces(rows, low_k + 3, high_k - 1))]
        crossing = send(sent, y_cross)
        given = [(a_low, a_pieces(low_k)), (a_high, a_pieces(high_k))]
        payloads = [((0, 0, rows),), ((1, rows, rows),)] if d == reach - 1 else []
        ends = use(given, *payloads)
        low, high = ends or (after(a_low, gathered[1]), after(a_high, gathered[1]))
        a_low, a_high = send(low, z_up), send(high, z_down)
    (sent,) = use(
        [(b_low, [(0, half, 1, far, 0)]), (b_high, [(0, half, 1, far, half)])],
        ((0, 0, half), (1, 0, half)),
    )
    last = send(sent, y_cross)
    use([(a_low, [(0, rows, 0, far, 0)]), (a_high, [(0, rows, 0, far + 1, 0)])])

    inputs = (ids, retrieval_ok, gain, queries, cotangent)
    attended, grad_a, slab, inv_a = forward(0, *inputs, *gathered, w_here)

    last_step = [grad_a]

    def back(grads, outs, arrays, *gates, dtype=jnp.bfloat16, cost=COST):
        held = [after(grad, last_step[0], *gates) for grad in grads]
        got = step(held, w_here, outs, arrays, dtype, cost)
        last_step[0] = got[0]
        return got

    crossed = {}

    def cross(d, *gates):
        ks = [2 * d + 1] if d == 0 else [2 * d + 1, 2 * (ring - d) + 1]
        outs = [[("sum", 0, 0, rows, k, []) for k in ks]]
        (got,) = back([grad_b], outs, [], *gates, cost=LIGHT if d == 0 else COST)
        got = send(got, y_cross)
        for i, k in enumerate(ks):
            crossed[k - 1] = (got, i * rows)
        return got

    def a_step(d, a_up, a_down):
        outs = []
        for arrived, k in ((0, 2 * d), (1, 2 * (ring - d))):
            own, other = [(arrived, 0)], [(arrived, rows)]
            if d == reach - 1:
                own, other = (own, []) if arrived == 0 else ([], [(1, 0)])
            outs.append([("sum", 0, 0, rows, k, own), ("sum", 0, 0, rows, k + 1, other)])
        if d > 1:
            a_up, a_down = back([grad_a], outs, [a_up, a_down])
            return send(a_up, z_up), send(a_down, z_down)
        parts = [[out[i]] for i in (1, 0) for out in outs]
        other_up, other_down, a_up, a_down = back([grad_a], parts, [a_up, a_down])
        other_up, other_down = send(other_up, z_up), send(other_down, z_down)
        a_up, a_down = send(a_up, z_up), send(a_down, z_down)
        return a_up, a_down, other_up, other_down

    def a_end(other_up, other_down):
        outs = [[("sum", 0, 0, rows, 1, [(0, 0), (1, 0)])]]
        return send(back([grad_a], outs, [other_up, other_down], cost=LIGHT)[0], y_cross)

    a_up, a_down = back(
        [grad_a], [[("sum", 0, 0, rows, far, [])], [("sum", 0, 0, rows, far + 1, [])]], []
    )
    made = a_up
    a_up, a_down = send(a_up, z_up), send(a_down, z_down)
    use(
        waiting
        + [(crossing, b_pieces(rows, far + 3, far - 1)), (last, [(0, rows, 1, far + 1, 0)])],
        gates=(made,),
        cost=LIGHT,
    )
    attended, grad_b, slab, inv_b = forward(1, *inputs, *gathered, w_here, attended, slab)
    last_step = [grad_b]
    (c_far,) = back(
        [grad_b],
        [[("sum", 0, 0, rows, far + 1, []), ("copy", 0, 0, SLAB)]],
        [slab],
        cost=LIGHT,
    )
    c_far = send(c_far, y_cross)
    a_up, a_down = a_step(reach - 1, a_up, a_down)
    c_last = cross(reach - 1)
    pair = ("pair", (0, 0), (1, rows))
    b_up, b_down = back(
        [grad_b],
        [
            [("sum", 0, 0, half, far, [(1, 0)]), pair],
            [("sum", 0, half, half, far, [(1, half)]), pair],
        ],
        [slab, c_far],
    )
    hops, slabs = [b_up], [(0, half)]
    height = half
    b_up, b_down = send(b_up, z_up), send(b_down, z_down)
    for d in range(reach - 1, 0, -1):
        c_last = cross(d - 1, c_last)
        hops += [b_up, b_down]
        slabs += [(len(hops) - 2, height), (len(hops) - 1, height)]
        arrays = [b_up, b_down, crossed[2 * d][0], crossed[2 * (ring - d)][0]]
        outs = []
        for i, k in ((0, 2 * d), (1, 2 * (ring - d))):
            at = crossed[k][1]
            if d == reach - 1:
                low, high = [(2 + i, at)], [(2 + i, at + half)]
                (low if i == 0 else high).append((i, 0))
                out = [("sum", 0, 0, half, k, low), ("sum", 0, half, half, k, high)]
            else:
                out = [("sum", 0, 0, rows, k, [(i, 0), (2 + i, at)])]
            outs.append(out + [("copy", i, height, SLAB)])
        b_up, b_down = back([grad_b], outs, arrays, cost=LIGHT if d == 1 else COST)
        b_up, b_down = send(b_up, z_up), send(b_down, z_down)
        height = rows
        if d > 1:
            a_up, a_down, *others = a_step(d - 1, a_up, a_down)
    swapped = a_end(*others)
    (before,) = back(
        [grad_a, grad_b],
        [[("sum", 0, 0, rows, 0, []), ("sum", 1, 0, rows, 0, [(0, 0)])]],
        [crossed[0][0]],
        dtype=jnp.float32,
        cost=LIGHT,
    )
    slabs = tuple((a + 4, r) for a, r in slabs) + ((3, rows),)
    share, far, ahead, behind, own = tail(
        ids, choose, gain, inv_a, inv_b, picked, before, swapped,
        [a_up, a_down, b_up, b_down] + hops, slabs, sections,
    )

    half = far.shape[0] // 2
    up = lax.ppermute(far[:half], "pipe", shift(sections, 1))
    down = lax.ppermute(far[half:], "pipe", shift(sections, -1))
    replicas = lax.axis_size("dp")
    share = share + lax.ppermute(share, "dp", [(i, i ^ 1) for i in range(replicas)])
    share = after(share, up)
    share = share + lax.ppermute(share, "dp", [(i, i ^ 2) for i in range(replicas)])
    ahead = jnp.concatenate([ahead[:half] + up, ahead[half:]], axis=0)
    behind = jnp.concatenate([behind[:half], behind[half:] + down], axis=0)
    up = lax.ppermute(bf16(ahead), "pipe", shift(sections, 1))
    down = lax.ppermute(bf16(behind), "pipe", shift(sections, -1))
    pool_grad = own + up + down
    return (attended, share, pool_grad)


def solution(mesh):
    return jax.shard_map(
        local,
        mesh=mesh,
        in_specs=(
            P(("pipe", "dp"), "tensor"),
            P(("pipe", "dp"), "tensor"),
            P(("pipe", "dp"), None),
            P(("pipe", "dp")),
            P("pipe", None),
            P("pipe", None, None, "tensor"),
            P(("pipe", "dp"), "tensor"),
        ),
        out_specs=(P(("pipe", "dp"), "tensor"), P("pipe", "tensor"), P(("pipe", "dp"), "tensor")),
        check_vma=False,
    )
```
